32 devices in a mesh: grp: 8 (over z, y), tp: 4 (over x, core).
Axes of the slice: x: 2, y: 2, z: 4, core: 2. Of those that a mesh axis runs over, the one named last changes fastest.
Arguments:
- gen_noise: bfloat16 [8, 256, 3072], P('grp'), may hold values from -6 to 6
- diff_noise: bfloat16 [8, 256, 3072], P('grp', 'tp'), may hold values from -6 to 6
- timesteps: int32 [8], P('grp'), may hold values from 0 to 15
- gen_mod: float32 [3, 3072], replicated, may hold values from -1 to 1
- teacher_mod: float32 [16, 3, 3072], replicated, may hold values from -1 to 1
- critic_mod: float32 [16, 3, 3072], replicated, may hold values from -1 to 1
- gen_up: bfloat16 [3072, 6144], P('grp', 'tp'), may hold values from -0.109375 to 0.109375
- gen_down: bfloat16 [6144, 3072], P('tp', 'grp'), may hold values from -0.078125 to 0.078125
- teacher_up: bfloat16 [3072, 6144], P(None, 'tp'), may hold values from -0.109375 to 0.109375
- teacher_down: bfloat16 [6144, 3072], P('tp'), may hold values from -0.078125 to 0.078125
- critic_up: bfloat16 [3072, 6144], P(None, 'tp'), may hold values from -0.109375 to 0.109375
- critic_down: bfloat16 [6144, 3072], P('tp'), may hold values from -0.078125 to 0.078125
Outputs:
- generated: bfloat16 [8, 256, 3072], P('grp', 'tp')
- up_grad: float32 [3072, 6144], P('grp', 'tp')
- down_grad: float32 [6144, 3072], P('tp', 'grp')
The draws below stay inside these ranges and needn't reach their ends.
All inputs are finite; a program needn't handle non-finite values.
Results may differ from the reference program's by a relative error of at most 0.0038.
Values may be sent and summed in bfloat16 or wider, within the bound.
No kernel may reach another device: no remote copies, remote signals or barrier semaphores. Data moves between devices by JAX's collectives and lax.ppermute only.
A program may use at most 192 MiB of HBM per device.

```python
import jax
import jax.numpy as jnp
from jax import lax

D = 3072
FF = 6144
LEVELS = 16
IMAGE_TOK = 256
SAMPLES = 8


def set_ends(drawn, key, least, top_value):
    spot = [jax.random.randint(jax.random.fold_in(key, axis), (), 0, length) for axis, length in enumerate(drawn.shape)]
    widest = drawn.shape.index(max(drawn.shape))
    neighbour = spot[:widest] + [(spot[widest] + 1) % drawn.shape[widest]] + spot[widest + 1:]
    return drawn.at[tuple(spot)].set(least).at[tuple(neighbour)].set(top_value)


def strengthened(values, key, source, target, blocks, factor):
    owner, partner = [(jnp.arange(values.shape[axis_at]) // (values.shape[axis_at] // blocks)).reshape([-1 if axis == axis_at else 1 for axis in range(values.ndim)]) for axis_at in (source, target)]
    chosen = jax.random.permutation(key, blocks)[partner]
    strong = (owner == chosen) | (owner == (partner + blocks // 2) % blocks)
    return jnp.where(strong, factor * values, values)


def levels(own_key, dims, shards, least, high):
    def one(position, blocks):
        heights = jax.random.uniform(jax.random.fold_in(jax.random.fold_in(own_key, 6), position), (blocks,), jnp.float32, least / len(shards), high / len(shards))
        return jnp.repeat(jnp.exp(heights), dims[position] // blocks).reshape((-1,) + (1,) * (len(dims) - position - 1))

    level = one(*shards[0])
    for cut in shards[1:]:
        level = level * one(*cut)
    return level


def bell_draw(rng, extent, width, reach, cuts=(), dtype=jnp.bfloat16):
    level = levels(rng, extent, cuts, -0.22, 0.18) if cuts else 1.0
    array = jax.random.normal(rng, extent, jnp.float32) * width * level
    return jnp.minimum(jnp.maximum(array, -reach), reach).astype(dtype)


def heavy_noise(own_key, extent, scale, reach, cuts, heavy, kind=jnp.bfloat16):
    result = scale * jax.random.normal(own_key, extent, jnp.float32)
    if cuts:
        result = result * levels(own_key, extent, cuts, -0.22, 0.18)
    return jnp.clip(strengthened(result, jax.random.fold_in(own_key, 3), *heavy), -reach, reach).astype(kind)


def setup_inputs(seed: int = 0) -> dict:
    seeds = jax.random.split(jax.random.key(seed), 13)
    return {
        "gen_noise": heavy_noise(seeds[0], (SAMPLES, IMAGE_TOK, D), 1.0, 6.0, ((0, 8),), (0, 2, 8, 2.0)),
        "diff_noise": bell_draw(seeds[1], (SAMPLES, IMAGE_TOK, D), 1.0, 6.0, ((0, 8), (1, 4))),
        "timesteps": set_ends(jax.random.randint(seeds[2], (SAMPLES,), 0, LEVELS), jax.random.fold_in(seeds[2], 1), 0, LEVELS - 1).astype(jnp.int32),
        "gen_mod": jnp.clip(jax.random.uniform(seeds[3], (3, D), jnp.float32, -1.0, 1.0), -1.0, 1.0),
        "teacher_mod": jnp.clip(jax.random.uniform(seeds[4], (LEVELS, 3, D), jnp.float32, -1.0, 1.0), -1.0, 1.0),
        "critic_mod": jnp.clip(jax.random.uniform(seeds[5], (LEVELS, 3, D), jnp.float32, -1.0, 1.0), -1.0, 1.0),
        "gen_up": bell_draw(seeds[6], (D, FF), D ** -0.5, 0.109375, ((0, 8), (1, 4))),
        "gen_down": bell_draw(seeds[7], (FF, D), FF ** -0.5, 0.078125, ((0, 4), (1, 8))),
        "teacher_up": bell_draw(seeds[8], (D, FF), D ** -0.5, 0.109375, ((1, 4),)),
        "teacher_down": bell_draw(seeds[9], (FF, D), FF ** -0.5, 0.078125, ((0, 4),)),
        "critic_up": bell_draw(seeds[10], (D, FF), D ** -0.5, 0.109375, ((1, 4),)),
        "critic_down": bell_draw(seeds[11], (FF, D), FF ** -0.5, 0.078125, ((0, 4),)),
    }


epsilon = 1e-06
root_two_pi = 0.7978845608028654
cubic = 0.044715

def normalize(values):
    center = values - lax.optimization_barrier(jnp.mean(values, axis=-1, keepdims=True))
    spread = lax.optimization_barrier(jnp.mean(center * center, axis=-1, keepdims=True))
    return center * lax.rsqrt(spread + epsilon)

def smooth_gate(values):
    inner = root_two_pi * (values + cubic * values * values * values)
    return 0.5 * values * (1.0 + jnp.tanh(inner))

def gate_slope(values):
    inner = root_two_pi * (values + cubic * values * values * values)
    tangent = jnp.tanh(inner)
    return 0.5 * (1.0 + tangent) + 0.5 * values * (1.0 - tangent * tangent) * root_two_pi * (1.0 + 3.0 * cubic * values * values)

def reference(gen_noise, diff_noise, timesteps, gen_mod, teacher_mod, critic_mod, gen_up, gen_down, teacher_up, teacher_down, critic_up, critic_down):
    total_rows = SAMPLES * IMAGE_TOK
    noise = gen_noise.astype(jnp.float32)
    gen_input = (normalize(noise) * (1.0 + gen_mod[1]) + gen_mod[0]).astype(jnp.bfloat16)
    flat_input = gen_input.reshape(total_rows, D)
    gen_pre = jnp.dot(flat_input, gen_up, preferred_element_type=jnp.float32)
    gen_hidden = smooth_gate(gen_pre).astype(jnp.bfloat16)
    gen_branch = jnp.dot(gen_hidden, gen_down, preferred_element_type=jnp.float32).reshape(SAMPLES, IMAGE_TOK, D)
    generated = (noise + gen_mod[2] * gen_branch).astype(jnp.bfloat16)
    level = (timesteps.astype(jnp.float32) + 1.0) / (LEVELS + 1)
    level_col = level[:, None, None]
    noised = ((1.0 - level_col) * generated.astype(jnp.float32) + level_col * diff_noise.astype(jnp.float32)).astype(jnp.bfloat16)
    normed = normalize(lax.optimization_barrier(noised).astype(jnp.float32))

    def score_branch(table, weight_up, weight_down):
        picked = table[timesteps]
        model_in = (normed * (1.0 + picked[:, 1:2]) + picked[:, 0:1]).astype(jnp.bfloat16).reshape(total_rows, D)
        hidden = smooth_gate(jnp.dot(model_in, weight_up, preferred_element_type=jnp.float32)).astype(jnp.bfloat16)
        summed = jnp.dot(hidden, weight_down, preferred_element_type=jnp.float32).reshape(SAMPLES, IMAGE_TOK, D)
        return picked[:, 2:3] * summed
    gap = level_col * (score_branch(teacher_mod, teacher_up, teacher_down) - score_branch(critic_mod, critic_up, critic_down))
    branch_grad = (gen_mod[2] * gap).astype(jnp.bfloat16).reshape(total_rows, D)
    down_grad = jnp.dot(gen_hidden.T, branch_grad, preferred_element_type=jnp.float32)
    hidden_grad = jnp.dot(branch_grad, gen_down.T, preferred_element_type=jnp.float32)
    pre_grad = (hidden_grad * gate_slope(gen_pre)).astype(jnp.bfloat16)
    up_grad = jnp.dot(flat_input.T, pre_grad, preferred_element_type=jnp.float32)
    return (generated, up_grad, down_grad)
```

```python
import jax
import jax.numpy as jnp
from jax import lax
from jax.sharding import PartitionSpec as P

epsilon = 1e-06
root_two_pi = 0.7978845608028654
cubic = 0.044715
f32 = jnp.float32
bf16 = jnp.bfloat16


def normalize(values):
    center = values - jnp.mean(values, axis=-1, keepdims=True)
    spread = jnp.mean(center * center, axis=-1, keepdims=True)
    return center * lax.rsqrt(spread + epsilon)


def smooth_gate(values):
    inner = root_two_pi * (values + cubic * values * values * values)
    return 0.5 * values * (1.0 + jnp.tanh(inner))


def gate_slope(values):
    inner = root_two_pi * (values + cubic * values * values * values)
    tangent = jnp.tanh(inner)
    return 0.5 * (1.0 + tangent) + 0.5 * values * (1.0 - tangent * tangent) * root_two_pi * (
        1.0 + 3.0 * cubic * values * values
    )


def pick_level(table, step_index):
    levels = lax.broadcasted_iota(jnp.int32, (table.shape[0], 1, 1), 0)
    return jnp.sum(jnp.where(levels == step_index, table, 0.0), axis=0)


def modulate(normed, picked):
    return (normed * (1.0 + picked[1]) + picked[0]).astype(bf16)


def dot(left, right, contract=((1,), (0,))):
    return lax.dot_general(left, right, (contract, ((), ())), preferred_element_type=f32)


def make_per_device(groups, parts):
    places = groups // 2
    ring_pairs = [(2 * p + s, 2 * ((p + 1) % places) + s) for p in range(places) for s in range(2)]
    swap_pairs = [(g, g ^ 1) for g in range(groups)]

    def ring(piece):
        return lax.ppermute(piece, "grp", ring_pairs)

    def swap(piece):
        return lax.ppermute(piece, "grp", swap_pairs)

    def gather_groups(own):
        near, far = [own], []
        for _ in range(places - 1):
            far.append(swap(near[-1]))
            near.append(ring(near[-1]))
        half = own.shape[0] // 2
        first = swap(near[-1][:half])
        second = ring(far[-1][half:]) if far else swap(near[-1][half:])
        far.append(jnp.concatenate([first, second], axis=0))
        return near, far

    def bit_pairs(bit):
        return [(t, t ^ (1 << bit)) for t in range(parts)]

    bits = parts.bit_length() - 1

    def sum_parts(values):
        place = lax.axis_index("tp")
        blocks = values.reshape(parts, values.shape[0] // parts, values.shape[1])
        for bit in range(bits):
            mine = (place >> bit) & 1
            split = blocks.reshape(blocks.shape[0] // 2, 2, *blocks.shape[1:])
            keep = lax.dynamic_index_in_dim(split, mine, 1, keepdims=False)
            send = lax.dynamic_index_in_dim(split, 1 - mine, 1, keepdims=False)
            if bit > 0:
                send = send.astype(bf16)
            blocks = keep + lax.ppermute(send, "tp", bit_pairs(bit)).astype(f32)
        return blocks[0]

    def gather_parts(values):
        place = lax.axis_index("tp")
        blocks = values[None]
        for bit in reversed(range(bits)):
            mine = (place >> bit) & 1
            other = lax.ppermute(blocks, "tp", bit_pairs(bit))
            pair = jnp.where(
                mine == 0, jnp.stack([blocks, other], 1), jnp.stack([other, blocks], 1)
            )
            blocks = pair.reshape(-1, *values.shape)
        return blocks

    def per_device(
        gen_noise,
        diff_noise,
        timesteps,
        gen_mod,
        teacher_mod,
        critic_mod,
        gen_up,
        gen_down,
        teacher_up,
        teacher_down,
        critic_up,
        critic_down,
    ):
        local_rows = diff_noise.shape[1]
        depth = gen_up.shape[0]
        step_index = timesteps[0]
        own = lax.axis_index("grp")
        place, side = own // 2, own % 2
        own_start = lax.axis_index("tp") * local_rows

        def origins():
            for k in range(places):
                yield lax.rem(place - k + places, places) * 2 + side
            for k in range(places):
                yield lax.rem(place - k + places, places) * 2 + 1 - side

        def to_absolute(near, far):
            order = [(-r) % places for r in range(places)]
            pairs = [
                jnp.where(
                    side == 0,
                    jnp.concatenate([near[k], far[k]], 1),
                    jnp.concatenate([far[k], near[k]], 1),
                )
                for k in order
            ]
            both = jnp.concatenate(pairs + pairs[:-1], 1)
            width = pairs[0].shape[1]
            start = lax.rem(places - place, places) * width
            return lax.dynamic_slice_in_dim(both, start, width * places, 1)

        noise_all = gen_noise[0].astype(f32)
        gen_rows = modulate(normalize(noise_all), gen_mod)
        noise = lax.dynamic_slice_in_dim(noise_all, own_start, local_rows, 0)

        up_near, up_far = gather_groups(gen_up)
        down_near, down_far = gather_groups(gen_down)

        gen_pre = None
        for piece, origin in zip(up_near + up_far, origins()):
            term = dot(lax.dynamic_slice_in_dim(gen_rows, origin * depth, depth, 1), piece)
            gen_pre = term if gen_pre is None else gen_pre + term
        gen_hidden = smooth_gate(gen_pre).astype(bf16)

        branch_near = [dot(gen_hidden, piece) for piece in down_near]
        branch_far = [dot(gen_hidden, piece) for piece in down_far]
        partial = to_absolute(branch_near, branch_far)
        gen_branch = sum_parts(partial)

        generated = (noise + gen_mod[2] * gen_branch).astype(bf16)
        level = (step_index.astype(f32) + 1.0) / (teacher_mod.shape[0] + 1)
        noised = (
            (1.0 - level) * generated.astype(f32) + level * diff_noise[0].astype(f32)
        ).astype(bf16)
        teacher_row = pick_level(teacher_mod, step_index)
        critic_row = pick_level(critic_mod, step_index)
        noised_all = gather_parts(lax.optimization_barrier(noised)).reshape(
            noise_all.shape
        )
        normed = normalize(noised_all.astype(f32))

        def score(row, weight_up, weight_down):
            hidden = smooth_gate(dot(modulate(normed, row), weight_up)).astype(bf16)
            return row[2] * dot(hidden, weight_down)

        gap_part = score(teacher_row, teacher_up, teacher_down) - score(
            critic_row, critic_up, critic_down
        )
        gap = level * sum_parts(gap_part)
        branch_grad = (gen_mod[2] * gap).astype(bf16)

        def own_columns(rows):
            count = rows.shape[0]
            blocks = rows.reshape(count, groups, depth).transpose(1, 0, 2)
            blocks = lax.all_to_all(blocks, "grp", 0, 0, tiled=True)
            return gather_parts(blocks).transpose(1, 0, 2, 3).reshape(groups, -1, depth)

        input_columns = own_columns(
            lax.dynamic_slice_in_dim(gen_rows, own_start, local_rows, 0)
        )
        grad_columns = own_columns(branch_grad)

        hidden_near, hidden_far = gather_groups(gen_hidden)
        down_grad = None
        for piece, origin in zip(hidden_near + hidden_far, origins()):
            columns = lax.dynamic_index_in_dim(grad_columns, origin, 0, keepdims=False)
            term = dot(piece, columns, ((0,), (0,)))
            down_grad = term if down_grad is None else down_grad + term

        piece_grad = gather_parts(branch_grad).reshape(noise_all.shape)
        hidden_grad = None
        for piece, origin in zip(down_near + down_far, origins()):
            columns = lax.dynamic_slice_in_dim(piece_grad, origin * depth, depth, 1)
            term = dot(columns, piece, ((1,), (1,)))
            hidden_grad = term if hidden_grad is None else hidden_grad + term
        rows_grad = (hidden_grad * gate_slope(gen_pre)).astype(bf16)

        grad_near, grad_far = gather_groups(rows_grad)
        up_grad = None
        for piece, origin in zip(grad_near + grad_far, origins()):
            columns = lax.dynamic_index_in_dim(input_columns, origin, 0, keepdims=False)
            term = dot(columns, piece, ((0,), (0,)))
            up_grad = term if up_grad is None else up_grad + term
        return (generated[None], up_grad, down_grad)

    return per_device


def solution(mesh):
    in_specs = (
        P("grp", None, None),
        P("grp", "tp", None),
        P("grp"),
        P(),
        P(),
        P(),
        P("grp", "tp"),
        P("tp", "grp"),
        P(None, "tp"),
        P("tp", None),
        P(None, "tp"),
        P("tp", None),
    )
    out_specs = (P("grp", "tp", None), P("grp", "tp"), P("tp", "grp"))
    return jax.shard_map(
        make_per_device(mesh.shape["grp"], mesh.shape["tp"]),
        mesh=mesh,
        in_specs=in_specs,
        out_specs=out_specs,
        check_vma=False,
    )
```

```python
import jax
import jax.numpy as jnp
from jax import lax
from jax.experimental import pallas as pl
from jax.experimental.pallas import tpu as pltpu
from jax.sharding import PartitionSpec as P

epsilon = 1e-06
root_two_pi = 0.7978845608028654
cubic = 0.044715
f32 = jnp.float32
bf16 = jnp.bfloat16


def normalize(values):
    center = values - jnp.mean(values, axis=-1, keepdims=True)
    spread = jnp.mean(center * center, axis=-1, keepdims=True)
    return center * lax.rsqrt(spread + epsilon)


def smooth_gate(values):
    inner = root_two_pi * (values + cubic * values * values * values)
    return 0.5 * values * (1.0 + jnp.tanh(inner))


def gate_slope(values):
    inner = root_two_pi * (values + cubic * values * values * values)
    tangent = jnp.tanh(inner)
    return 0.5 * (1.0 + tangent) + 0.5 * values * (1.0 - tangent * tangent) * root_two_pi * (
        1.0 + 3.0 * cubic * values * values
    )


def pick_level(table, step_index):
    levels = lax.broadcasted_iota(jnp.int32, (table.shape[0], 1, 1), 0)
    return jnp.sum(jnp.where(levels == step_index, table, 0.0), axis=0)


def modulate(normed, picked):
    return (normed * (1.0 + picked[1]) + picked[0]).astype(bf16)


def dot(left, right, contract=((1,), (0,))):
    return lax.dot_general(left, right, (contract, ((), ())), preferred_element_type=f32)


def make_ring(groups, parts):
    places = groups // 2
    ring_pairs = [(2 * p + s, 2 * ((p + 1) % places) + s) for p in range(places) for s in range(2)]
    swap_pairs = [(g, g ^ 1) for g in range(groups)]

    def ring(piece):
        return lax.ppermute(piece, "grp", ring_pairs)

    def swap(piece):
        return lax.ppermute(piece, "grp", swap_pairs)

    def gather_groups(own):
        near, far = [own], []
        for _ in range(places - 1):
            far.append(swap(near[-1]))
            near.append(ring(near[-1]))
        half = own.shape[0] // 2
        first = swap(near[-1][:half])
        second = ring(far[-1][half:]) if far else swap(near[-1][half:])
        far.append(jnp.concatenate([first, second], axis=0))
        return near, far

    def bit_pairs(bit):
        return [(t, t ^ (1 << bit)) for t in range(parts)]

    bits = parts.bit_length() - 1

    def sum_parts(values):
        place = lax.axis_index("tp")
        blocks = values.reshape(parts, values.shape[0] // parts, values.shape[1])
        for bit in range(bits):
            mine = (place >> bit) & 1
            split = blocks.reshape(blocks.shape[0] // 2, 2, *blocks.shape[1:])
            keep = lax.dynamic_index_in_dim(split, mine, 1, keepdims=False)
            send = lax.dynamic_index_in_dim(split, 1 - mine, 1, keepdims=False)
            if bit > 0:
                send = send.astype(bf16)
            blocks = keep + lax.ppermute(send, "tp", bit_pairs(bit)).astype(f32)
        return blocks[0]

    def gather_parts(values):
        place = lax.axis_index("tp")
        blocks = values[None]
        for bit in reversed(range(bits)):
            mine = (place >> bit) & 1
            other = lax.ppermute(blocks, "tp", bit_pairs(bit))
            pair = jnp.where(
                mine == 0, jnp.stack([blocks, other], 1), jnp.stack([other, blocks], 1)
            )
            blocks = pair.reshape(-1, *values.shape)
        return blocks

    def per_device(
        gen_noise,
        diff_noise,
        timesteps,
        gen_mod,
        teacher_mod,
        critic_mod,
        gen_up,
        gen_down,
        teacher_up,
        teacher_down,
        critic_up,
        critic_down,
    ):
        local_rows = diff_noise.shape[1]
        depth = gen_up.shape[0]
        step_index = timesteps[0]
        own = lax.axis_index("grp")
        place, side = own // 2, own % 2
        own_start = lax.axis_index("tp") * local_rows

        def origins():
            for k in range(places):
                yield lax.rem(place - k + places, places) * 2 + side
            for k in range(places):
                yield lax.rem(place - k + places, places) * 2 + 1 - side

        def to_absolute(near, far):
            order = [(-r) % places for r in range(places)]
            pairs = [
                jnp.where(
                    side == 0,
                    jnp.concatenate([near[k], far[k]], 1),
                    jnp.concatenate([far[k], near[k]], 1),
                )
                for k in order
            ]
            both = jnp.concatenate(pairs + pairs[:-1], 1)
            width = pairs[0].shape[1]
            start = lax.rem(places - place, places) * width
            return lax.dynamic_slice_in_dim(both, start, width * places, 1)

        noise_all = gen_noise[0].astype(f32)
        gen_rows = modulate(normalize(noise_all), gen_mod)
        noise = lax.dynamic_slice_in_dim(noise_all, own_start, local_rows, 0)

        up_near, up_far = gather_groups(gen_up)
        down_near, down_far = gather_groups(gen_down)

        gen_pre = None
        for piece, origin in zip(up_near + up_far, origins()):
            term = dot(lax.dynamic_slice_in_dim(gen_rows, origin * depth, depth, 1), piece)
            gen_pre = term if gen_pre is None else gen_pre + term
        gen_hidden = smooth_gate(gen_pre).astype(bf16)

        branch_near = [dot(gen_hidden, piece) for piece in down_near]
        branch_far = [dot(gen_hidden, piece) for piece in down_far]
        partial = to_absolute(branch_near, branch_far)
        gen_branch = sum_parts(partial)

        generated = (noise + gen_mod[2] * gen_branch).astype(bf16)
        level = (step_index.astype(f32) + 1.0) / (teacher_mod.shape[0] + 1)
        noised = (
            (1.0 - level) * generated.astype(f32) + level * diff_noise[0].astype(f32)
        ).astype(bf16)
        teacher_row = pick_level(teacher_mod, step_index)
        critic_row = pick_level(critic_mod, step_index)
        noised_all = gather_parts(lax.optimization_barrier(noised)).reshape(
            noise_all.shape
        )
        normed = normalize(noised_all.astype(f32))

        def score(row, weight_up, weight_down):
            hidden = smooth_gate(dot(modulate(normed, row), weight_up)).astype(bf16)
            return row[2] * dot(hidden, weight_down)

        gap_part = score(teacher_row, teacher_up, teacher_down) - score(
            critic_row, critic_up, critic_down
        )
        gap = level * sum_parts(gap_part)
        branch_grad = (gen_mod[2] * gap).astype(bf16)

        def own_columns(rows):
            count = rows.shape[0]
            blocks = rows.reshape(count, groups, depth).transpose(1, 0, 2)
            blocks = lax.all_to_all(blocks, "grp", 0, 0, tiled=True)
            return gather_parts(blocks).transpose(1, 0, 2, 3).reshape(groups, -1, depth)

        input_columns = own_columns(
            lax.dynamic_slice_in_dim(gen_rows, own_start, local_rows, 0)
        )
        grad_columns = own_columns(branch_grad)

        hidden_near, hidden_far = gather_groups(gen_hidden)
        down_grad = None
        for piece, origin in zip(hidden_near + hidden_far, origins()):
            columns = lax.dynamic_index_in_dim(grad_columns, origin, 0, keepdims=False)
            term = dot(piece, columns, ((0,), (0,)))
            down_grad = term if down_grad is None else down_grad + term

        piece_grad = gather_parts(branch_grad).reshape(noise_all.shape)
        hidden_grad = None
        for piece, origin in zip(down_near + down_far, origins()):
            columns = lax.dynamic_slice_in_dim(piece_grad, origin * depth, depth, 1)
            term = dot(columns, piece, ((1,), (1,)))
            hidden_grad = term if hidden_grad is None else hidden_grad + term
        rows_grad = (hidden_grad * gate_slope(gen_pre)).astype(bf16)

        grad_near, grad_far = gather_groups(rows_grad)
        up_grad = None
        for piece, origin in zip(grad_near + grad_far, origins()):
            columns = lax.dynamic_index_in_dim(input_columns, origin, 0, keepdims=False)
            term = dot(columns, piece, ((0,), (0,)))
            up_grad = term if up_grad is None else up_grad + term
        return (generated[None], up_grad, down_grad)

    return per_device


def kernel_call(body, out_shapes, *operands, scalars=None, name, flops=0, moved=None):
    specs = [pl.BlockSpec(memory_space=pltpu.VMEM) for _ in operands]
    if scalars is not None:
        operands = (scalars, *operands)
        specs = [pl.BlockSpec(memory_space=pltpu.SMEM), *specs]
    total = sum(o.size * o.dtype.itemsize for o in operands)
    total += sum(o.size * jnp.dtype(o.dtype).itemsize for o in out_shapes)
    return pl.pallas_call(
        body,
        out_shape=tuple(out_shapes),
        in_specs=specs,
        out_specs=tuple(pl.BlockSpec(memory_space=pltpu.VMEM) for _ in out_shapes),
        compiler_params=pltpu.CompilerParams(vmem_limit_bytes=48 * 1024 * 1024),
        cost_estimate=pl.CostEstimate(flops=flops, bytes_accessed=total, transcendentals=0),
        name=name,
    )(*operands)


def settle(*arrays):
    def body(*refs):
        pass

    return pl.pallas_call(
        body,
        out_shape=tuple(jax.ShapeDtypeStruct(a.shape, a.dtype) for a in arrays),
        in_specs=[pl.BlockSpec(memory_space=pl.ANY) for _ in arrays],
        out_specs=tuple(pl.BlockSpec(memory_space=pl.ANY) for _ in arrays),
        input_output_aliases={i: i for i in range(len(arrays))},
        name="settle",
    )(*arrays)


def make_paired(groups, parts):
    pair, swap, far = 2, 1, 4
    core, side = 1, 2
    order = (0, side, core, core | side)
    masks = range(groups)

    def hop(values, axis, mask):
        size = groups if axis == "grp" else parts
        return lax.ppermute(values, axis, [(i, i ^ mask) for i in range(size)])

    def shape(*dims, dtype=bf16):
        return jax.ShapeDtypeStruct(dims, dtype)

    def gather_tokens(own):
        crossed = hop(own, "tp", side)
        return [own, crossed, hop(own, "tp", core), hop(crossed, "tp", core)]

    ring_pairs = [(g, (g + 2) % groups) for g in range(groups)]

    def ring(values):
        return lax.ppermute(values, "grp", ring_pairs)

    def send_blocks(blocks, mask):
        return hop(blocks[:, blocks.shape[1] // 2 :], "grp", mask)

    def with_arrived(blocks, arrived):
        return jnp.concatenate([blocks[:, : blocks.shape[1] // 2], arrived], 0)

    def own_columns(tokens, scalars):
        _, rows, depth = tokens[0].shape

        def body(s, *refs):
            for g in masks:
                for at, image_index in enumerate((g, g ^ pair)):
                    m = s[0] ^ image_index
                    spot = (m & pair) + (m & 1) * 4 + (m // 4)
                    for k, ref in enumerate(refs[:-1]):
                        start = (at * parts + k) * rows
                        refs[-1][g, start : start + rows, :] = ref[spot]

        (packed,) = kernel_call(
            body,
            [shape(groups, 2 * parts * rows, depth)],
            *tokens,
            scalars=scalars,
            name="pack",
        )
        return packed

    def per_device(
        gen_noise,
        diff_noise,
        timesteps,
        gen_mod,
        teacher_mod,
        critic_mod,
        gen_up,
        gen_down,
        teacher_up,
        teacher_down,
        critic_up,
        critic_down,
    ):
        rows = diff_noise.shape[1]
        image = gen_noise.shape[1]
        depth = gen_up.shape[0]
        width = gen_noise.shape[2]
        units = gen_up.shape[1] // 2
        middle = width // 2
        score_units = teacher_up.shape[1]
        level_count = teacher_mod.shape[0] + 1.0
        own = lax.axis_index("grp")
        part = lax.axis_index("tp")
        half = (own // pair) % 2
        scalars = jnp.stack([own, part, timesteps[0], half])

        def block(ref_own, m):
            return pl.ds(pl.multiple_of((ref_own ^ m) * depth, 128), depth)

        def fixed(m):
            return slice(m * depth, (m + 1) * depth)

        def halves(values, axis):
            return tuple(
                lax.dynamic_slice_in_dim(values, index * units, units, axis)
                for index in (half, 1 - half)
            )

        up, down = {}, {}
        up[0], up_send = halves(gen_up, 1)
        down[0], down_send = halves(gen_down, 0)

        def input_body(s, noise_ref, mod_ref, rows_ref, blocks_ref):
            for k, mask in enumerate(order):
                start = pl.multiple_of((s[1] ^ mask) * rows, 16)
                values = noise_ref[0, pl.ds(start, rows), :].astype(f32)
                values = normalize(values) * (1.0 + mod_ref[1:2]) + mod_ref[0:1]
                rows_ref[k * rows : (k + 1) * rows, :] = values.astype(bf16)
            for m in masks:
                blocks_ref[m] = rows_ref[:rows, block(s[0], m)]

        up[pair] = hop(up_send, "grp", pair)
        up[far] = hop(up[0], "grp", far)
        up[swap] = hop(up[0], "grp", swap)
        gen_rows, input_blocks = kernel_call(
            input_body,
            [shape(image, width), shape(groups, rows, depth)],
            gen_noise,
            gen_mod,
            scalars=scalars,
            name="input",
        )
        (
            up[pair],
            up[far],
            up[swap],
            down_send,
            gen_rows,
            input_blocks,
        ) = settle(up[pair], up[far], up[swap], down_send, gen_rows, input_blocks)
        up[pair | far] = hop(up[pair], "grp", far)
        up[pair | swap] = hop(up[pair], "grp", swap)
        up[far | swap] = hop(up[far], "grp", swap)
        down[pair] = hop(down_send, "grp", pair)
        pair_rows = gather_tokens(hop(gen_rows[:rows], "grp", pair))
        (
            up[pair | far],
            up[pair | swap],
            up[far | swap],
            down[pair],
            down[0],
        ) = settle(up[pair | far], up[pair | swap], up[far | swap], down[pair], down[0])
        up[pair | far | swap] = hop(up[pair | far], "grp", swap)
        down[far] = hop(down[0], "grp", far)
        down[swap] = hop(down[0], "grp", swap)
        up[pair | far | swap], down[pair], down[far], down[swap] = settle(
            up[pair | far | swap], down[pair], down[far], down[swap]
        )
        down[pair | far] = hop(down[pair], "grp", far)
        down[pair | swap] = hop(down[pair], "grp", swap)
        down[far | swap] = hop(down[far], "grp", swap)

        def pre_body(s, rows_ref, p0, p1, p2, p3, *refs):
            pieces, (pre_ref, hidden_ref) = refs[:groups], refs[groups:]
            for m in masks:
                spot = block(s[0], m)
                left = jnp.concatenate(
                    [rows_ref[:, spot]] + [p[:, spot] for p in (p0, p1, p2, p3)], 0
                )
                term = dot(left, pieces[m][...])
                if m == 0:
                    pre_ref[...] = term
                else:
                    pre_ref[...] += term
            hidden_ref[...] = smooth_gate(pre_ref[...]).astype(bf16)

        gen_pre, gen_hidden = kernel_call(
            pre_body,
            [shape(2 * image, units, dtype=f32), shape(2 * image, units)],
            gen_rows,
            *pair_rows,
            *[up[m] for m in masks],
            scalars=scalars,
            name="pre",
            flops=4 * image * width * units,
        )

        down[pair | far], down[pair | swap], down[far | swap], gen_hidden = settle(
            down[pair | far], down[pair | swap], down[far | swap], gen_hidden
        )
        down[pair | far | swap] = hop(down[pair | far], "grp", swap)
        down[pair | far | swap], gen_hidden, input_blocks = settle(
            down[pair | far | swap], gen_hidden, input_blocks[None]
        )
        hidden_near, hidden_across = [gen_hidden], [hop(gen_hidden, "grp", swap)]
        arrived = send_blocks(input_blocks, far)

        def branch_body(hidden_ref, *refs):
            pieces, (keep_ref, send_ref) = refs[:-2], refs[-2:]
            for m, piece in enumerate(pieces):
                for image_at, spot in ((0, m), (1, m ^ pair)):
                    values = dot(
                        hidden_ref[image_at * image : (image_at + 1) * image, :], piece[...]
                    )
                    cut = slice(image_at * image // 2, (image_at + 1) * image // 2)
                    keep_ref[cut, fixed(spot)] = values[: image // 2]
                    send_ref[cut, fixed(spot)] = values[image // 2 :].astype(bf16)

        def core_body(keep_ref, got_ref, first_ref, second_ref, third_ref, rest_ref):
            def total(at):
                cut = slice(at * rows, (at + 1) * rows)
                return keep_ref[cut, :] + got_ref[cut, :].astype(f32)

            first_ref[...] = total(3).astype(bf16)
            second_ref[...] = total(1).astype(bf16)
            third_ref[...] = total(2)
            rest_ref[...] = total(0)

        def add_body(left_ref, right_ref, out_ref):
            out_ref[...] = (left_ref[...] + right_ref[...].astype(f32)).astype(bf16)

        def branch_sum(which):
            count = groups // 2
            keep, send = kernel_call(
                branch_body,
                [shape(image, middle, dtype=f32), shape(image, middle)],
                gen_hidden,
                *[down[m] for m in masks if m // count == which],
                name="branch",
                flops=2 * image * width * units,
            )
            first, second, third, rest = kernel_call(
                core_body,
                [shape(rows, middle)] * 2 + [shape(rows, middle, dtype=f32)] * 2,
                keep,
                hop(send, "tp", core),
                name="core_sum",
            )
            (third,) = kernel_call(
                add_body,
                [shape(rows, middle)],
                third,
                hop(first, "tp", side),
                name="side_sum",
            )
            return rest, hop(second, "tp", side), hop(third, "grp", pair)

        def latent_body(s, noise_ref, diff_ref, mod_ref, *refs):
            sums, (generated_ref, noised_ref) = refs[:6], refs[6:]
            level = (s[2].astype(f32) + 1.0) / level_count
            start = pl.multiple_of(s[1] * rows, 16)
            for m in masks:
                which, at = divmod(m, groups // 2)
                a, b, c = sums[3 * which : 3 * which + 3]
                branch = (
                    a[:, fixed(at)] + b[:, fixed(at)].astype(f32) + c[:, fixed(at)].astype(f32)
                )
                spot = block(s[0], m)
                noise = noise_ref[0, pl.ds(start, rows), spot].astype(f32)
                made = (noise + mod_ref[2:3, spot] * branch).astype(bf16)
                generated_ref[0, :, spot] = made
                noised_ref[:, spot] = (
                    (1.0 - level) * made.astype(f32) + level * diff_ref[0, :, spot].astype(f32)
                ).astype(bf16)

        left_sum = branch_sum(0)
        right_sum = branch_sum(1)
        generated, noised = kernel_call(
            latent_body,
            [shape(1, rows, width), shape(rows, width)],
            gen_noise,
            diff_noise,
            gen_mod,
            *left_sum,
            *right_sum,
            scalars=scalars,
            name="latent",
        )

        noised, hidden_near[0], hidden_across[0], arrived = settle(
            noised, hidden_near[0], hidden_across[0], arrived
        )
        hidden_near.append(ring(hidden_near[0]))
        input_blocks = with_arrived(input_blocks, arrived)
        arrived = send_blocks(input_blocks, pair)

        def score_input_body(s, n0, n1, n2, n3, teacher_ref, critic_ref, t_ref, c_ref):
            for k, part_ref in enumerate((n0, n1, n2, n3)):
                normed = normalize(part_ref[...].astype(f32))
                cut = slice(k * rows, (k + 1) * rows)
                for table, out in ((teacher_ref, t_ref), (critic_ref, c_ref)):
                    row = table[s[2]]
                    out[cut, :] = (normed * (1.0 + row[1:2]) + row[0:1]).astype(bf16)

        teacher_in, critic_in = kernel_call(
            score_input_body,
            [shape(image, width)] * 2,
            *gather_tokens(noised),
            teacher_mod,
            critic_mod,
            scalars=scalars,
            name="score_input",
        )

        teacher_in, hidden_near[1], arrived = settle(teacher_in, hidden_near[1], arrived)
        hidden_near.append(ring(hidden_near[1]))
        hidden_across.append(hop(hidden_near[1], "grp", swap))
        input_blocks = with_arrived(input_blocks, arrived)
        arrived = send_blocks(input_blocks, swap)

        tile = 256

        def hidden_body(t_in, c_in, t_w, c_w, t_out, c_out):
            t_out[...] = smooth_gate(dot(t_in[...], t_w[...])).astype(bf16)
            c_out[...] = smooth_gate(dot(c_in[...], c_w[...])).astype(bf16)

        whole = pl.BlockSpec((image, width), lambda j: (0, 0))
        teacher_hidden, critic_hidden = pl.pallas_call(
            hidden_body,
            grid=(score_units // tile,),
            in_specs=[whole, whole] + [pl.BlockSpec((width, tile), lambda j: (0, j))] * 2,
            out_specs=[pl.BlockSpec((image, tile), lambda j: (0, j))] * 2,
            out_shape=[shape(image, score_units)] * 2,
            compiler_params=pltpu.CompilerParams(vmem_limit_bytes=48 * 1024 * 1024),
            cost_estimate=pl.CostEstimate(
                flops=4 * image * width * score_units,
                bytes_accessed=4 * width * score_units,
                transcendentals=0,
            ),
            name="score_hidden",
        )(teacher_in, critic_in, teacher_up, critic_up)

        def gap_body(s, t_h, c_h, t_w, c_w, t_mod, c_mod, keep_ref, send_ref):
            values = t_mod[s[2], 2:3] * dot(t_h[...], t_w[...]) - c_mod[s[2], 2:3] * dot(
                c_h[...], c_w[...]
            )
            keep_ref[...] = values[: image // 2]
            send_ref[...] = values[image // 2 :].astype(bf16)

        whole = pl.BlockSpec((image, score_units), lambda j: (0, 0))
        keep, send = pl.pallas_call(
            gap_body,
            grid=(width // tile,),
            in_specs=[pl.BlockSpec(memory_space=pltpu.SMEM), whole, whole]
            + [pl.BlockSpec((score_units, tile), lambda j: (0, j))] * 2
            + [pl.BlockSpec((*teacher_mod.shape[:2], tile), lambda j: (0, 0, j))] * 2,
            out_specs=[pl.BlockSpec((image // 2, tile), lambda j: (0, j))] * 2,
            out_shape=[shape(image // 2, width, dtype=f32), shape(image // 2, width)],
            compiler_params=pltpu.CompilerParams(vmem_limit_bytes=48 * 1024 * 1024),
            cost_estimate=pl.CostEstimate(
                flops=4 * image * width * score_units,
                bytes_accessed=4 * width * score_units,
                transcendentals=0,
            ),
            name="score_gap",
        )(scalars, teacher_hidden, critic_hidden, teacher_down, critic_down, teacher_mod, critic_mod)

        send, hidden_near[2], hidden_across[1], arrived = settle(
            send, hidden_near[2], hidden_across[1], arrived
        )
        hidden_near.append(ring(hidden_near[2]))
        hidden_across.append(hop(hidden_near[2], "grp", swap))
        input_blocks = with_arrived(input_blocks, arrived)

        def gap_core_body(keep_ref, got_ref, send_ref, rest_ref):
            send_ref[...] = (keep_ref[rows:, :] + got_ref[rows:, :].astype(f32)).astype(bf16)
            rest_ref[...] = keep_ref[:rows, :] + got_ref[:rows, :].astype(f32)

        send, rest = kernel_call(
            gap_core_body,
            [shape(rows, width), shape(rows, width, dtype=f32)],
            keep,
            hop(send, "tp", core),
            name="gap_core",
        )

        def grad_body(s, rest_ref, got_ref, mod_ref, rows_ref, blocks_ref):
            level = (s[2].astype(f32) + 1.0) / level_count
            for m in masks:
                spot = block(s[0], m)
                gap = level * (rest_ref[:, spot] + got_ref[:, spot].astype(f32))
                values = (mod_ref[2:3, spot] * gap).astype(bf16)
                rows_ref[:, fixed(m)] = values
                blocks_ref[m] = values

        branch_grad, grad_blocks = kernel_call(
            grad_body,
            [shape(rows, width), shape(groups, rows, depth)],
            rest,
            hop(send, "tp", side),
            gen_mod,
            scalars=scalars,
            name="branch_grad",
        )

        branch_grad, hidden_near[3], hidden_across[2], grad_blocks = settle(
            branch_grad, hidden_near[3], hidden_across[2], grad_blocks[None]
        )
        pair_grad = hop(branch_grad, "grp", pair)
        crossed = hop(branch_grad, "tp", side)
        arrived = send_blocks(grad_blocks, far)
        pair_grad, crossed, arrived = settle(pair_grad, crossed, arrived)
        grad_blocks = with_arrived(grad_blocks, arrived)
        own_tokens = [branch_grad, crossed]
        own_tokens += [hop(values, "tp", core) for values in own_tokens]
        pair_tokens = gather_tokens(pair_grad)
        arrived = send_blocks(grad_blocks, pair)
        pair_tokens[-1], arrived = settle(pair_tokens[-1], arrived)
        grad_blocks = with_arrived(grad_blocks, arrived)
        arrived = send_blocks(grad_blocks, swap)
        hidden_last = [
            hop(hidden_near[-1][:image], "grp", swap),
            ring(hidden_across[-1][image:]),
        ]

        def rows_grad_body(*refs):
            tokens, pieces = refs[:8], refs[8 : 8 + groups]
            pre_ref, out_ref, total = refs[8 + groups :]
            for m in masks:
                left = jnp.concatenate(
                    [t[:, fixed(m)] for t in tokens[:4]]
                    + [t[:, fixed(m ^ pair)] for t in tokens[4:]],
                    0,
                )
                term = dot(left, pieces[m][...], ((1,), (1,)))
                if m == 0:
                    total[...] = term
                else:
                    total[...] += term
            out_ref[...] = (total[...] * gate_slope(pre_ref[...])).astype(bf16)

        operands = (*own_tokens, *pair_tokens, *[down[m] for m in masks], gen_pre)
        rows_grad = pl.pallas_call(
            rows_grad_body,
            out_shape=shape(2 * image, units),
            in_specs=[pl.BlockSpec(memory_space=pltpu.VMEM) for _ in operands],
            out_specs=pl.BlockSpec(memory_space=pltpu.VMEM),
            scratch_shapes=[pltpu.VMEM((2 * image, units), f32)],
            compiler_params=pltpu.CompilerParams(vmem_limit_bytes=48 * 1024 * 1024),
            cost_estimate=pl.CostEstimate(
                flops=4 * image * width * units, bytes_accessed=10**7, transcendentals=0
            ),
            name="rows_grad",
        )(*operands)

        rows_grad, arrived, input_blocks, *hidden_last = settle(
            rows_grad, arrived, input_blocks, *hidden_last
        )
        grad_blocks = with_arrived(grad_blocks, arrived)
        near, across = [rows_grad], []
        for k in range(groups // 2 - 1):
            near.append(ring(near[k]))
            across.append(hop(near[k], "grp", swap))
        input_columns = own_columns(gather_tokens(input_blocks[:, 0]), scalars)
        grad_columns = own_columns(gather_tokens(grad_blocks[:, 0]), scalars)

        def columns_at(table, k, other):
            origin = lax.rem(own + groups - 2 * k, groups) ^ other
            return lax.dynamic_index_in_dim(table, origin, 0, keepdims=False)

        def in_order(table, near, across, last=()):
            for k, piece in enumerate(near):
                yield k % 2, columns_at(table, k, 0), piece
            for k, piece in enumerate(across):
                yield k % 2, columns_at(table, k, swap), piece
            for at, piece in enumerate(last):
                columns = columns_at(table, groups // 2 - 1, swap)
                yield 1, columns[at * image : (at + 1) * image], piece

        def over_tokens(left, right):
            return dot(left, right, ((0,), (0,)))

        def join_halves(mine, other, axis):
            return jnp.where(
                half == 0,
                jnp.concatenate([mine, other], axis),
                jnp.concatenate([other, mine], axis),
            )

        down_sums = [0.0, 0.0]
        for which, columns, piece in in_order(
            grad_columns, hidden_near, hidden_across, hidden_last
        ):
            down_sums[which] += over_tokens(piece, columns)
        near[-1], across[-1], *down_sums = settle(near[-1], across[-1], *down_sums)
        last = [hop(near[-1][:image], "grp", swap), ring(across[-1][image:])]
        up_sums = [0.0, 0.0]
        for which, columns, piece in in_order(input_columns, near, across, last):
            up_sums[which] += over_tokens(columns, piece)
        return generated, join_halves(*up_sums, 1), join_halves(*down_sums, 0)

    return per_device


def make_per_device(groups, parts):
    def per_device(*args):
        depth, units = args[6].shape
        fits = depth % 128 == 0 and units % 512 == 0 and args[1].shape[1] % 16 == 0
        if groups == 8 and parts == 4 and fits:
            return make_paired(groups, parts)(*args)
        return make_ring(groups, parts)(*args)

    return per_device


def solution(mesh):
    in_specs = (
        P("grp", None, None),
        P("grp", "tp", None),
        P("grp"),
        P(),
        P(),
        P(),
        P("grp", "tp"),
        P("tp", "grp"),
        P(None, "tp"),
        P("tp", None),
        P(None, "tp"),
        P("tp", None),
    )
    out_specs = (P("grp", "tp", None), P("grp", "tp"), P("tp", "grp"))
    return jax.shard_map(
        make_per_device(mesh.shape["grp"], mesh.shape["tp"]),
        mesh=mesh,
        in_specs=in_specs,
        out_specs=out_specs,
        check_vma=False,
    )
```

```python
import jax
import jax.numpy as jnp
from jax import lax
from jax.experimental import pallas as pl
from jax.experimental.pallas import tpu as pltpu
from jax.sharding import PartitionSpec as P

epsilon = 1e-06
root_two_pi = 0.7978845608028654
cubic = 0.044715
f32 = jnp.float32
bf16 = jnp.bfloat16


def normalize(values):
    center = values - jnp.mean(values, axis=-1, keepdims=True)
    spread = jnp.mean(center * center, axis=-1, keepdims=True)
    return center * lax.rsqrt(spread + epsilon)


def smooth_gate(values):
    inner = root_two_pi * (values + cubic * values * values * values)
    return 0.5 * values * (1.0 + jnp.tanh(inner))


def gate_slope(values):
    inner = root_two_pi * (values + cubic * values * values * values)
    tangent = jnp.tanh(inner)
    return 0.5 * (1.0 + tangent) + 0.5 * values * (1.0 - tangent * tangent) * root_two_pi * (
        1.0 + 3.0 * cubic * values * values
    )


def pick_level(table, step_index):
    levels = lax.broadcasted_iota(jnp.int32, (table.shape[0], 1, 1), 0)
    return jnp.sum(jnp.where(levels == step_index, table, 0.0), axis=0)


def modulate(normed, picked):
    return (normed * (1.0 + picked[1]) + picked[0]).astype(bf16)


def dot(left, right, contract=((1,), (0,))):
    return lax.dot_general(left, right, (contract, ((), ())), preferred_element_type=f32)


def make_ring(groups, parts):
    places = groups // 2
    ring_pairs = [(2 * p + s, 2 * ((p + 1) % places) + s) for p in range(places) for s in range(2)]
    swap_pairs = [(g, g ^ 1) for g in range(groups)]

    def ring(piece):
        return lax.ppermute(piece, "grp", ring_pairs)

    def swap(piece):
        return lax.ppermute(piece, "grp", swap_pairs)

    def gather_groups(own):
        near, far = [own], []
        for _ in range(places - 1):
            far.append(swap(near[-1]))
            near.append(ring(near[-1]))
        half = own.shape[0] // 2
        first = swap(near[-1][:half])
        second = ring(far[-1][half:]) if far else swap(near[-1][half:])
        far.append(jnp.concatenate([first, second], axis=0))
        return near, far

    def bit_pairs(bit):
        return [(t, t ^ (1 << bit)) for t in range(parts)]

    bits = parts.bit_length() - 1

    def sum_parts(values):
        place = lax.axis_index("tp")
        blocks = values.reshape(parts, values.shape[0] // parts, values.shape[1])
        for bit in range(bits):
            mine = (place >> bit) & 1
            split = blocks.reshape(blocks.shape[0] // 2, 2, *blocks.shape[1:])
            keep = lax.dynamic_index_in_dim(split, mine, 1, keepdims=False)
            send = lax.dynamic_index_in_dim(split, 1 - mine, 1, keepdims=False)
            if bit > 0:
                send = send.astype(bf16)
            blocks = keep + lax.ppermute(send, "tp", bit_pairs(bit)).astype(f32)
        return blocks[0]

    def gather_parts(values):
        place = lax.axis_index("tp")
        blocks = values[None]
        for bit in reversed(range(bits)):
            mine = (place >> bit) & 1
            other = lax.ppermute(blocks, "tp", bit_pairs(bit))
            pair = jnp.where(
                mine == 0, jnp.stack([blocks, other], 1), jnp.stack([other, blocks], 1)
            )
            blocks = pair.reshape(-1, *values.shape)
        return blocks

    def per_device(
        gen_noise,
        diff_noise,
        timesteps,
        gen_mod,
        teacher_mod,
        critic_mod,
        gen_up,
        gen_down,
        teacher_up,
        teacher_down,
        critic_up,
        critic_down,
    ):
        local_rows = diff_noise.shape[1]
        depth = gen_up.shape[0]
        step_index = timesteps[0]
        own = lax.axis_index("grp")
        place, side = own // 2, own % 2
        own_start = lax.axis_index("tp") * local_rows

        def origins():
            for k in range(places):
                yield lax.rem(place - k + places, places) * 2 + side
            for k in range(places):
                yield lax.rem(place - k + places, places) * 2 + 1 - side

        def to_absolute(near, far):
            order = [(-r) % places for r in range(places)]
            pairs = [
                jnp.where(
                    side == 0,
                    jnp.concatenate([near[k], far[k]], 1),
                    jnp.concatenate([far[k], near[k]], 1),
                )
                for k in order
            ]
            both = jnp.concatenate(pairs + pairs[:-1], 1)
            width = pairs[0].shape[1]
            start = lax.rem(places - place, places) * width
            return lax.dynamic_slice_in_dim(both, start, width * places, 1)

        noise_all = gen_noise[0].astype(f32)
        gen_rows = modulate(normalize(noise_all), gen_mod)
        noise = lax.dynamic_slice_in_dim(noise_all, own_start, local_rows, 0)

        up_near, up_far = gather_groups(gen_up)
        down_near, down_far = gather_groups(gen_down)

        gen_pre = None
        for piece, origin in zip(up_near + up_far, origins()):
            term = dot(lax.dynamic_slice_in_dim(gen_rows, origin * depth, depth, 1), piece)
            gen_pre = term if gen_pre is None else gen_pre + term
        gen_hidden = smooth_gate(gen_pre).astype(bf16)

        branch_near = [dot(gen_hidden, piece) for piece in down_near]
        branch_far = [dot(gen_hidden, piece) for piece in down_far]
        partial = to_absolute(branch_near, branch_far)
        gen_branch = sum_parts(partial)

        generated = (noise + gen_mod[2] * gen_branch).astype(bf16)
        level = (step_index.astype(f32) + 1.0) / (teacher_mod.shape[0] + 1)
        noised = (
            (1.0 - level) * generated.astype(f32) + level * diff_noise[0].astype(f32)
        ).astype(bf16)
        teacher_row = pick_level(teacher_mod, step_index)
        critic_row = pick_level(critic_mod, step_index)
        noised_all = gather_parts(lax.optimization_barrier(noised)).reshape(
            noise_all.shape
        )
        normed = normalize(noised_all.astype(f32))

        def score(row, weight_up, weight_down):
            hidden = smooth_gate(dot(modulate(normed, row), weight_up)).astype(bf16)
            return row[2] * dot(hidden, weight_down)

        gap_part = score(teacher_row, teacher_up, teacher_down) - score(
            critic_row, critic_up, critic_down
        )
        gap = level * sum_parts(gap_part)
        branch_grad = (gen_mod[2] * gap).astype(bf16)

        def own_columns(rows):
            count = rows.shape[0]
            blocks = rows.reshape(count, groups, depth).transpose(1, 0, 2)
            blocks = lax.all_to_all(blocks, "grp", 0, 0, tiled=True)
            return gather_parts(blocks).transpose(1, 0, 2, 3).reshape(groups, -1, depth)

        input_columns = own_columns(
            lax.dynamic_slice_in_dim(gen_rows, own_start, local_rows, 0)
        )
        grad_columns = own_columns(branch_grad)

        hidden_near, hidden_far = gather_groups(gen_hidden)
        down_grad = None
        for piece, origin in zip(hidden_near + hidden_far, origins()):
            columns = lax.dynamic_index_in_dim(grad_columns, origin, 0, keepdims=False)
            term = dot(piece, columns, ((0,), (0,)))
            down_grad = term if down_grad is None else down_grad + term

        piece_grad = gather_parts(branch_grad).reshape(noise_all.shape)
        hidden_grad = None
        for piece, origin in zip(down_near + down_far, origins()):
            columns = lax.dynamic_slice_in_dim(piece_grad, origin * depth, depth, 1)
            term = dot(columns, piece, ((1,), (1,)))
            hidden_grad = term if hidden_grad is None else hidden_grad + term
        rows_grad = (hidden_grad * gate_slope(gen_pre)).astype(bf16)

        grad_near, grad_far = gather_groups(rows_grad)
        up_grad = None
        for piece, origin in zip(grad_near + grad_far, origins()):
            columns = lax.dynamic_index_in_dim(input_columns, origin, 0, keepdims=False)
            term = dot(columns, piece, ((0,), (0,)))
            up_grad = term if up_grad is None else up_grad + term
        return (generated[None], up_grad, down_grad)

    return per_device


def kernel_call(body, out_shapes, *operands, scalars=None, name, flops=0, moved=None):
    specs = [pl.BlockSpec(memory_space=pltpu.VMEM) for _ in operands]
    if scalars is not None:
        operands = (scalars, *operands)
        specs = [pl.BlockSpec(memory_space=pltpu.SMEM), *specs]
    total = sum(o.size * o.dtype.itemsize for o in operands)
    total += sum(o.size * jnp.dtype(o.dtype).itemsize for o in out_shapes)
    return pl.pallas_call(
        body,
        out_shape=tuple(out_shapes),
        in_specs=specs,
        out_specs=tuple(pl.BlockSpec(memory_space=pltpu.VMEM) for _ in out_shapes),
        compiler_params=pltpu.CompilerParams(vmem_limit_bytes=8 * 1024 * 1024),
        cost_estimate=pl.CostEstimate(flops=flops, bytes_accessed=total, transcendentals=0),
        name=name,
    )(*operands)


def settle(*arrays):
    def body(*refs):
        pass

    return pl.pallas_call(
        body,
        out_shape=tuple(jax.ShapeDtypeStruct(a.shape, a.dtype) for a in arrays),
        in_specs=[pl.BlockSpec(memory_space=pl.ANY) for _ in arrays],
        out_specs=tuple(pl.BlockSpec(memory_space=pl.ANY) for _ in arrays),
        input_output_aliases={i: i for i in range(len(arrays))},
        compiler_params=pltpu.CompilerParams(vmem_limit_bytes=256 * 1024),
        name="settle",
    )(*arrays)


def make_paired(groups, parts):
    pair, swap, far = 2, 1, 4
    core, side = 1, 2
    order = (0, side, core, core | side)
    masks = range(groups)

    def hop(values, axis, mask):
        size = groups if axis == "grp" else parts
        return lax.ppermute(values, axis, [(i, i ^ mask) for i in range(size)])

    def shape(*dims, dtype=bf16):
        return jax.ShapeDtypeStruct(dims, dtype)

    def gather_tokens(own):
        crossed = hop(own, "tp", side)
        return [own, crossed, hop(own, "tp", core), hop(crossed, "tp", core)]

    ring_pairs = [(g, (g + 2) % groups) for g in range(groups)]

    def ring(values):
        return lax.ppermute(values, "grp", ring_pairs)

    def send_blocks(blocks, mask):
        return hop(blocks[:, blocks.shape[1] // 2 :], "grp", mask)

    def with_arrived(blocks, arrived):
        return jnp.concatenate([blocks[:, : blocks.shape[1] // 2], arrived], 0)

    def own_columns(tokens, scalars):
        _, rows, depth = tokens[0].shape

        def body(s, *refs):
            for g in masks:
                for at, image_index in enumerate((g, g ^ pair)):
                    m = s[0] ^ image_index
                    spot = (m & pair) + (m & 1) * 4 + (m // 4)
                    for k, ref in enumerate(refs[:-1]):
                        start = (at * parts + k) * rows
                        refs[-1][g, start : start + rows, :] = ref[spot]

        (packed,) = kernel_call(
            body,
            [shape(groups, 2 * parts * rows, depth)],
            *tokens,
            scalars=scalars,
            name="pack",
        )
        return packed

    def per_device(
        gen_noise,
        diff_noise,
        timesteps,
        gen_mod,
        teacher_mod,
        critic_mod,
        gen_up,
        gen_down,
        teacher_up,
        teacher_down,
        critic_up,
        critic_down,
    ):
        rows = diff_noise.shape[1]
        image = gen_noise.shape[1]
        depth = gen_up.shape[0]
        width = gen_noise.shape[2]
        units = gen_up.shape[1] // 2
        middle = width // 2
        score_units = teacher_up.shape[1]
        level_count = teacher_mod.shape[0] + 1.0
        own = lax.axis_index("grp")
        part = lax.axis_index("tp")
        half = (own // pair) % 2
        scalars = jnp.stack([own, part, timesteps[0], half])

        def block(ref_own, m):
            return pl.ds(pl.multiple_of((ref_own ^ m) * depth, 128), depth)

        def fixed(m):
            return slice(m * depth, (m + 1) * depth)

        def halves(values, axis):
            return tuple(
                lax.dynamic_slice_in_dim(values, index * units, units, axis)
                for index in (half, 1 - half)
            )

        up, down = {}, {}
        up[0], up_send = halves(gen_up, 1)
        down[0], down_send = halves(gen_down, 0)

        def input_body(s, noise_ref, mod_ref, rows_ref, blocks_ref):
            for k, mask in enumerate(order):
                start = pl.multiple_of((s[1] ^ mask) * rows, 16)
                values = noise_ref[0, pl.ds(start, rows), :].astype(f32)
                values = normalize(values) * (1.0 + mod_ref[1:2]) + mod_ref[0:1]
                rows_ref[k * rows : (k + 1) * rows, :] = values.astype(bf16)
            for m in masks:
                blocks_ref[m] = rows_ref[:rows, block(s[0], m)]

        up[pair] = hop(up_send, "grp", pair)
        up[far] = hop(up[0], "grp", far)
        up[swap] = hop(up[0], "grp", swap)
        gen_rows, input_blocks = kernel_call(
            input_body,
            [shape(image, width), shape(groups, rows, depth)],
            gen_noise,
            gen_mod,
            scalars=scalars,
            name="input",
        )
        (
            up[pair],
            up[far],
            up[swap],
            down_send,
            gen_rows,
            input_blocks,
        ) = settle(up[pair], up[far], up[swap], down_send, gen_rows, input_blocks)
        up[pair | far] = hop(up[pair], "grp", far)
        up[pair | swap] = hop(up[pair], "grp", swap)
        up[far | swap] = hop(up[far], "grp", swap)
        down[pair] = hop(down_send, "grp", pair)
        pair_rows = gather_tokens(hop(gen_rows[:rows], "grp", pair))
        (
            up[pair | far],
            up[pair | swap],
            up[far | swap],
            down[pair],
            down[0],
        ) = settle(up[pair | far], up[pair | swap], up[far | swap], down[pair], down[0])
        up[pair | far | swap] = hop(up[pair | far], "grp", swap)
        down[far] = hop(down[0], "grp", far)
        down[swap] = hop(down[0], "grp", swap)
        up[pair | far | swap], down[pair], down[far], down[swap] = settle(
            up[pair | far | swap], down[pair], down[far], down[swap]
        )
        down[pair | far] = hop(down[pair], "grp", far)
        down[pair | swap] = hop(down[pair], "grp", swap)
        down[far | swap] = hop(down[far], "grp", swap)

        def pre_body(s, rows_ref, p0, p1, p2, p3, *refs):
            pieces, (pre_ref, hidden_ref) = refs[:groups], refs[groups:]
            for m in masks:
                spot = block(s[0], m)
                left = jnp.concatenate(
                    [rows_ref[:, spot]] + [p[:, spot] for p in (p0, p1, p2, p3)], 0
                )
                term = dot(left, pieces[m][...])
                if m == 0:
                    pre_ref[...] = term
                else:
                    pre_ref[...] += term
            hidden_ref[...] = smooth_gate(pre_ref[...]).astype(bf16)

        gen_pre, gen_hidden = kernel_call(
            pre_body,
            [shape(2 * image, units, dtype=f32), shape(2 * image, units)],
            gen_rows,
            *pair_rows,
            *[up[m] for m in masks],
            scalars=scalars,
            name="pre",
            flops=4 * image * width * units,
        )

        def branch_body(hidden_ref, *refs):
            pieces, (keep_ref, send_ref) = refs[:-2], refs[-2:]
            for m, piece in enumerate(pieces):
                for image_at, spot in ((0, m), (1, m ^ pair)):
                    values = dot(
                        hidden_ref[image_at * image : (image_at + 1) * image, :], piece[...]
                    )
                    cut = slice(image_at * image // 2, (image_at + 1) * image // 2)
                    keep_ref[cut, fixed(spot)] = values[: image // 2]
                    send_ref[cut, fixed(spot)] = values[image // 2 :].astype(bf16)

        def core_body(keep_ref, got_ref, first_ref, second_ref, third_ref, rest_ref):
            def total(at):
                cut = slice(at * rows, (at + 1) * rows)
                return keep_ref[cut, :] + got_ref[cut, :].astype(f32)

            first_ref[...] = total(3).astype(bf16)
            second_ref[...] = total(1).astype(bf16)
            third_ref[...] = total(2)
            rest_ref[...] = total(0)

        def add_body(left_ref, right_ref, out_ref):
            out_ref[...] = (left_ref[...] + right_ref[...].astype(f32)).astype(bf16)

        def branch_core(which, hidden):
            count = groups // 2
            keep, send = kernel_call(
                branch_body,
                [shape(image, middle, dtype=f32), shape(image, middle)],
                hidden,
                *[down[m] for m in masks if m // count == which],
                name="branch",
                flops=2 * image * width * units,
            )
            return kernel_call(
                core_body,
                [shape(rows, middle)] * 2 + [shape(rows, middle, dtype=f32)] * 2,
                keep,
                hop(send, "tp", core),
                name="core_sum",
            )

        def branch_sum(first, second, third, rest):
            (third,) = kernel_call(
                add_body,
                [shape(rows, middle)],
                third,
                hop(first, "tp", side),
                name="side_sum",
            )
            return rest, hop(second, "tp", side), hop(third, "grp", pair)

        (
            down[pair | far],
            down[pair | swap],
            down[far | swap],
            gen_hidden,
            input_blocks,
        ) = settle(
            down[pair | far],
            down[pair | swap],
            down[far | swap],
            gen_hidden,
            input_blocks[None],
        )
        down[pair | far | swap] = hop(down[pair | far], "grp", swap)
        arrived = send_blocks(input_blocks, far)
        left_terms = branch_core(0, gen_hidden)
        down[pair | far | swap], gen_hidden, arrived, *left_terms = settle(
            down[pair | far | swap], gen_hidden, arrived, *left_terms
        )
        left_sum = branch_sum(*left_terms)
        hidden_near, hidden_across = [gen_hidden], [hop(gen_hidden, "grp", swap)]
        input_blocks = with_arrived(input_blocks, arrived)
        arrived = send_blocks(input_blocks, pair)
        right_terms = branch_core(1, gen_hidden)
        arrived, *right_terms = settle(arrived, *right_terms)
        right_sum = branch_sum(*right_terms)
        input_blocks = with_arrived(input_blocks, arrived)
        arrived = send_blocks(input_blocks, swap)

        def latent_body(s, noise_ref, diff_ref, mod_ref, *refs):
            sums, (generated_ref, noised_ref) = refs[:6], refs[6:]
            level = (s[2].astype(f32) + 1.0) / level_count
            start = pl.multiple_of(s[1] * rows, 16)
            for m in masks:
                which, at = divmod(m, groups // 2)
                a, b, c = sums[3 * which : 3 * which + 3]
                branch = (
                    a[:, fixed(at)] + b[:, fixed(at)].astype(f32) + c[:, fixed(at)].astype(f32)
                )
                spot = block(s[0], m)
                noise = noise_ref[0, pl.ds(start, rows), spot].astype(f32)
                made = (noise + mod_ref[2:3, spot] * branch).astype(bf16)
                generated_ref[0, :, spot] = made
                noised_ref[:, spot] = (
                    (1.0 - level) * made.astype(f32) + level * diff_ref[0, :, spot].astype(f32)
                ).astype(bf16)

        generated, noised = kernel_call(
            latent_body,
            [shape(1, rows, width), shape(rows, width)],
            gen_noise,
            diff_noise,
            gen_mod,
            *left_sum,
            *right_sum,
            scalars=scalars,
            name="latent",
        )

        noised, hidden_near[0], hidden_across[0], arrived = settle(
            noised, hidden_near[0], hidden_across[0], arrived
        )
        hidden_near.append(ring(hidden_near[0]))

        def score_input_body(s, n0, n1, n2, n3, teacher_ref, critic_ref, t_ref, c_ref):
            for k, part_ref in enumerate((n0, n1, n2, n3)):
                normed = normalize(part_ref[...].astype(f32))
                cut = slice(k * rows, (k + 1) * rows)
                for table, out in ((teacher_ref, t_ref), (critic_ref, c_ref)):
                    row = table[s[2]]
                    out[cut, :] = (normed * (1.0 + row[1:2]) + row[0:1]).astype(bf16)

        teacher_in, critic_in = kernel_call(
            score_input_body,
            [shape(image, width)] * 2,
            *gather_tokens(noised),
            teacher_mod,
            critic_mod,
            scalars=scalars,
            name="score_input",
        )

        teacher_in, arrived = settle(teacher_in, arrived)
        input_tokens = gather_tokens(with_arrived(input_blocks, arrived)[:, 0])

        tile = 256

        def hidden_body(t_in, c_in, t_w, c_w, t_out, c_out):
            t_out[...] = smooth_gate(dot(t_in[...], t_w[...])).astype(bf16)
            c_out[...] = smooth_gate(dot(c_in[...], c_w[...])).astype(bf16)

        whole = pl.BlockSpec((image, width), lambda j: (0, 0))
        teacher_hidden, critic_hidden = pl.pallas_call(
            hidden_body,
            grid=(score_units // tile,),
            in_specs=[whole, whole] + [pl.BlockSpec((width, tile), lambda j: (0, j))] * 2,
            out_specs=[pl.BlockSpec((image, tile), lambda j: (0, j))] * 2,
            out_shape=[shape(image, score_units)] * 2,
            compiler_params=pltpu.CompilerParams(vmem_limit_bytes=8 * 1024 * 1024),
            cost_estimate=pl.CostEstimate(
                flops=4 * image * width * score_units,
                bytes_accessed=4 * width * score_units,
                transcendentals=0,
            ),
            name="score_hidden",
        )(teacher_in, critic_in, teacher_up, critic_up)

        teacher_hidden, hidden_near[1], *input_tokens = settle(
            teacher_hidden, hidden_near[1], *input_tokens
        )
        hidden_near.append(ring(hidden_near[1]))
        hidden_across.append(hop(hidden_near[1], "grp", swap))

        def gap_body(s, t_h, c_h, t_w, c_w, t_mod, c_mod, keep_ref, send_ref):
            values = t_mod[s[2], 2:3] * dot(t_h[...], t_w[...]) - c_mod[s[2], 2:3] * dot(
                c_h[...], c_w[...]
            )
            keep_ref[...] = values[: image // 2]
            send_ref[...] = values[image // 2 :].astype(bf16)

        whole = pl.BlockSpec((image, score_units), lambda j: (0, 0))
        keep, send = pl.pallas_call(
            gap_body,
            grid=(width // tile,),
            in_specs=[pl.BlockSpec(memory_space=pltpu.SMEM), whole, whole]
            + [pl.BlockSpec((score_units, tile), lambda j: (0, j))] * 2
            + [pl.BlockSpec((*teacher_mod.shape[:2], tile), lambda j: (0, 0, j))] * 2,
            out_specs=[pl.BlockSpec((image // 2, tile), lambda j: (0, j))] * 2,
            out_shape=[shape(image // 2, width, dtype=f32), shape(image // 2, width)],
            compiler_params=pltpu.CompilerParams(vmem_limit_bytes=8 * 1024 * 1024),
            cost_estimate=pl.CostEstimate(
                flops=4 * image * width * score_units,
                bytes_accessed=4 * width * score_units,
                transcendentals=0,
            ),
            name="score_gap",
        )(scalars, teacher_hidden, critic_hidden, teacher_down, critic_down, teacher_mod, critic_mod)

        send, hidden_near[2], hidden_across[1] = settle(
            send, hidden_near[2], hidden_across[1]
        )
        hidden_near.append(ring(hidden_near[2]))
        hidden_across.append(hop(hidden_near[2], "grp", swap))

        def gap_core_body(keep_ref, got_ref, send_ref, rest_ref):
            send_ref[...] = (keep_ref[rows:, :] + got_ref[rows:, :].astype(f32)).astype(bf16)
            rest_ref[...] = keep_ref[:rows, :] + got_ref[:rows, :].astype(f32)

        send, rest = kernel_call(
            gap_core_body,
            [shape(rows, width), shape(rows, width, dtype=f32)],
            keep,
            hop(send, "tp", core),
            name="gap_core",
        )

        def grad_body(s, rest_ref, got_ref, mod_ref, rows_ref, blocks_ref):
            level = (s[2].astype(f32) + 1.0) / level_count
            for m in masks:
                spot = block(s[0], m)
                gap = level * (rest_ref[:, spot] + got_ref[:, spot].astype(f32))
                values = (mod_ref[2:3, spot] * gap).astype(bf16)
                rows_ref[:, fixed(m)] = values
                blocks_ref[m] = values

        branch_grad, grad_blocks = kernel_call(
            grad_body,
            [shape(rows, width), shape(groups, rows, depth)],
            rest,
            hop(send, "tp", side),
            gen_mod,
            scalars=scalars,
            name="branch_grad",
        )

        grad_blocks = grad_blocks[None]
        pair_grad = hop(branch_grad, "grp", pair)
        crossed = hop(branch_grad, "tp", side)
        arrived = send_blocks(grad_blocks, far)
        pair_grad, crossed, arrived, hidden_near[3], hidden_across[2] = settle(
            pair_grad, crossed, arrived, hidden_near[3], hidden_across[2]
        )
        hidden_across.append(hop(hidden_near[3], "grp", swap))
        pair_crossed = hop(pair_grad, "tp", side)
        own_tokens = [branch_grad, crossed]
        own_tokens += [hop(values, "tp", core) for values in own_tokens]
        grad_blocks = with_arrived(grad_blocks, arrived)
        arrived = send_blocks(grad_blocks, pair)
        pair_core = hop(pair_grad, "tp", core)
        pair_crossed, arrived = settle(pair_crossed, arrived)
        pair_tokens = [pair_grad, pair_crossed, pair_core, hop(pair_crossed, "tp", core)]

        def rows_grad_body(*refs):
            tokens, pieces = refs[:8], refs[8 : 8 + groups]
            pre_ref, out_ref, total = refs[8 + groups :]
            for m in masks:
                left = jnp.concatenate(
                    [t[:, fixed(m)] for t in tokens[:4]]
                    + [t[:, fixed(m ^ pair)] for t in tokens[4:]],
                    0,
                )
                term = dot(left, pieces[m][...], ((1,), (1,)))
                if m == 0:
                    total[...] = term
                else:
                    total[...] += term
            out_ref[...] = (total[...] * gate_slope(pre_ref[...])).astype(bf16)

        operands = (*own_tokens, *pair_tokens, *[down[m] for m in masks], gen_pre)
        rows_grad = pl.pallas_call(
            rows_grad_body,
            out_shape=shape(2 * image, units),
            in_specs=[pl.BlockSpec(memory_space=pltpu.VMEM) for _ in operands],
            out_specs=pl.BlockSpec(memory_space=pltpu.VMEM),
            scratch_shapes=[pltpu.VMEM((2 * image, units), f32)],
            compiler_params=pltpu.CompilerParams(vmem_limit_bytes=8 * 1024 * 1024),
            cost_estimate=pl.CostEstimate(
                flops=4 * image * width * units, bytes_accessed=10**7, transcendentals=0
            ),
            name="rows_grad",
        )(*operands)

        rows_grad, arrived, hidden_across[3] = settle(rows_grad, arrived, hidden_across[3])
        near, across = [rows_grad, ring(rows_grad)], [hop(rows_grad, "grp", swap)]
        grad_blocks = with_arrived(grad_blocks, arrived)
        arrived = send_blocks(grad_blocks, swap)
        near[1], across[0], arrived = settle(near[1], across[0], arrived)
        near.append(ring(near[1]))
        across.append(hop(near[1], "grp", swap))
        grad_tokens = gather_tokens(with_arrived(grad_blocks, arrived)[:, 0])
        near[2], across[1], *grad_tokens = settle(near[2], across[1], *grad_tokens)
        near.append(ring(near[2]))
        across.append(hop(near[2], "grp", swap))
        input_columns = own_columns(input_tokens, scalars)
        grad_columns = own_columns(grad_tokens, scalars)

        def columns_at(table, k, other):
            origin = lax.rem(own + groups - 2 * k, groups) ^ other
            return lax.dynamic_index_in_dim(table, origin, 0, keepdims=False)

        def in_order(table, near, across, last=()):
            for k, piece in enumerate(near):
                yield k % 2, columns_at(table, k, 0), piece
            for k, piece in enumerate(across):
                yield k % 2, columns_at(table, k, swap), piece
            for at, piece in enumerate(last):
                columns = columns_at(table, groups // 2 - 1, swap)
                yield 1, columns[at * image : (at + 1) * image], piece

        def over_tokens(left, right):
            return dot(left, right, ((0,), (0,)))

        def join_halves(mine, other, axis):
            return jnp.where(
                half == 0,
                jnp.concatenate([mine, other], axis),
                jnp.concatenate([other, mine], axis),
            )

        down_sums = [0.0, 0.0]
        for which, columns, piece in in_order(
            grad_columns, hidden_near, hidden_across
        ):
            down_sums[which] += over_tokens(piece, columns)
        near[-1], across[-1], *down_sums = settle(near[-1], across[-1], *down_sums)
        last = [hop(near[-1][:image], "grp", swap), ring(across[-1][image:])]
        up_sums = [0.0, 0.0]
        for which, columns, piece in in_order(input_columns, near, across, last):
            up_sums[which] += over_tokens(columns, piece)
        return generated, join_halves(*up_sums, 1), join_halves(*down_sums, 0)

    return per_device


def make_per_device(groups, parts):
    def per_device(*args):
        depth, units = args[6].shape
        fits = depth % 128 == 0 and units % 512 == 0 and args[1].shape[1] % 16 == 0
        if groups == 8 and parts == 4 and fits:
            return make_paired(groups, parts)(*args)
        return make_ring(groups, parts)(*args)

    return per_device


def solution(mesh):
    in_specs = (
        P("grp", None, None),
        P("grp", "tp", None),
        P("grp"),
        P(),
        P(),
        P(),
        P("grp", "tp"),
        P("tp", "grp"),
        P(None, "tp"),
        P("tp", None),
        P(None, "tp"),
        P("tp", None),
    )
    out_specs = (P("grp", "tp", None), P("grp", "tp"), P("tp", "grp"))
    return jax.shard_map(
        make_per_device(mesh.shape["grp"], mesh.shape["tp"]),
        mesh=mesh,
        in_specs=in_specs,
        out_specs=out_specs,
        check_vma=False,
    )
```

```python
import jax
import jax.numpy as jnp
from jax import lax
from jax.experimental import pallas as pl
from jax.experimental.pallas import tpu as pltpu
from jax.sharding import PartitionSpec as P

epsilon = 1e-06
root_two_pi = 0.7978845608028654
cubic = 0.044715
f32 = jnp.float32
bf16 = jnp.bfloat16


def normalize(values):
    center = values - jnp.mean(values, axis=-1, keepdims=True)
    spread = jnp.mean(center * center, axis=-1, keepdims=True)
    return center * lax.rsqrt(spread + epsilon)


def smooth_gate(values):
    inner = root_two_pi * (values + cubic * values * values * values)
    return 0.5 * values * (1.0 + jnp.tanh(inner))


def gate_slope(values):
    inner = root_two_pi * (values + cubic * values * values * values)
    tangent = jnp.tanh(inner)
    return 0.5 * (1.0 + tangent) + 0.5 * values * (1.0 - tangent * tangent) * root_two_pi * (
        1.0 + 3.0 * cubic * values * values
    )


def pick_level(table, step_index):
    levels = lax.broadcasted_iota(jnp.int32, (table.shape[0], 1, 1), 0)
    return jnp.sum(jnp.where(levels == step_index, table, 0.0), axis=0)


def modulate(normed, picked):
    return (normed * (1.0 + picked[1]) + picked[0]).astype(bf16)


def dot(left, right, contract=((1,), (0,))):
    return lax.dot_general(left, right, (contract, ((), ())), preferred_element_type=f32)


def make_ring(groups, parts):
    places = groups // 2
    ring_pairs = [(2 * p + s, 2 * ((p + 1) % places) + s) for p in range(places) for s in range(2)]
    swap_pairs = [(g, g ^ 1) for g in range(groups)]

    def ring(piece):
        return lax.ppermute(piece, "grp", ring_pairs)

    def swap(piece):
        return lax.ppermute(piece, "grp", swap_pairs)

    def gather_groups(own):
        near, far = [own], []
        for _ in range(places - 1):
            far.append(swap(near[-1]))
            near.append(ring(near[-1]))
        half = own.shape[0] // 2
        first = swap(near[-1][:half])
        second = ring(far[-1][half:]) if far else swap(near[-1][half:])
        far.append(jnp.concatenate([first, second], axis=0))
        return near, far

    def bit_pairs(bit):
        return [(t, t ^ (1 << bit)) for t in range(parts)]

    bits = parts.bit_length() - 1

    def sum_parts(values):
        place = lax.axis_index("tp")
        blocks = values.reshape(parts, values.shape[0] // parts, values.shape[1])
        for bit in range(bits):
            mine = (place >> bit) & 1
            split = blocks.reshape(blocks.shape[0] // 2, 2, *blocks.shape[1:])
            keep = lax.dynamic_index_in_dim(split, mine, 1, keepdims=False)
            send = lax.dynamic_index_in_dim(split, 1 - mine, 1, keepdims=False)
            if bit > 0:
                send = send.astype(bf16)
            blocks = keep + lax.ppermute(send, "tp", bit_pairs(bit)).astype(f32)
        return blocks[0]

    def gather_parts(values):
        place = lax.axis_index("tp")
        blocks = values[None]
        for bit in reversed(range(bits)):
            mine = (place >> bit) & 1
            other = lax.ppermute(blocks, "tp", bit_pairs(bit))
            pair = jnp.where(
                mine == 0, jnp.stack([blocks, other], 1), jnp.stack([other, blocks], 1)
            )
            blocks = pair.reshape(-1, *values.shape)
        return blocks

    def per_device(
        gen_noise,
        diff_noise,
        timesteps,
        gen_mod,
        teacher_mod,
        critic_mod,
        gen_up,
        gen_down,
        teacher_up,
        teacher_down,
        critic_up,
        critic_down,
    ):
        local_rows = diff_noise.shape[1]
        depth = gen_up.shape[0]
        step_index = timesteps[0]
        own = lax.axis_index("grp")
        place, side = own // 2, own % 2
        own_start = lax.axis_index("tp") * local_rows

        def origins():
            for k in range(places):
                yield lax.rem(place - k + places, places) * 2 + side
            for k in range(places):
                yield lax.rem(place - k + places, places) * 2 + 1 - side

        def to_absolute(near, far):
            order = [(-r) % places for r in range(places)]
            pairs = [
                jnp.where(
                    side == 0,
                    jnp.concatenate([near[k], far[k]], 1),
                    jnp.concatenate([far[k], near[k]], 1),
                )
                for k in order
            ]
            both = jnp.concatenate(pairs + pairs[:-1], 1)
            width = pairs[0].shape[1]
            start = lax.rem(places - place, places) * width
            return lax.dynamic_slice_in_dim(both, start, width * places, 1)

        noise_all = gen_noise[0].astype(f32)
        gen_rows = modulate(normalize(noise_all), gen_mod)
        noise = lax.dynamic_slice_in_dim(noise_all, own_start, local_rows, 0)

        up_near, up_far = gather_groups(gen_up)
        down_near, down_far = gather_groups(gen_down)

        gen_pre = None
        for piece, origin in zip(up_near + up_far, origins()):
            term = dot(lax.dynamic_slice_in_dim(gen_rows, origin * depth, depth, 1), piece)
            gen_pre = term if gen_pre is None else gen_pre + term
        gen_hidden = smooth_gate(gen_pre).astype(bf16)

        branch_near = [dot(gen_hidden, piece) for piece in down_near]
        branch_far = [dot(gen_hidden, piece) for piece in down_far]
        partial = to_absolute(branch_near, branch_far)
        gen_branch = sum_parts(partial)

        generated = (noise + gen_mod[2] * gen_branch).astype(bf16)
        level = (step_index.astype(f32) + 1.0) / (teacher_mod.shape[0] + 1)
        noised = (
            (1.0 - level) * generated.astype(f32) + level * diff_noise[0].astype(f32)
        ).astype(bf16)
        teacher_row = pick_level(teacher_mod, step_index)
        critic_row = pick_level(critic_mod, step_index)
        noised_all = gather_parts(lax.optimization_barrier(noised)).reshape(
            noise_all.shape
        )
        normed = normalize(noised_all.astype(f32))

        def score(row, weight_up, weight_down):
            hidden = smooth_gate(dot(modulate(normed, row), weight_up)).astype(bf16)
            return row[2] * dot(hidden, weight_down)

        gap_part = score(teacher_row, teacher_up, teacher_down) - score(
            critic_row, critic_up, critic_down
        )
        gap = level * sum_parts(gap_part)
        branch_grad = (gen_mod[2] * gap).astype(bf16)

        def own_columns(rows):
            count = rows.shape[0]
            blocks = rows.reshape(count, groups, depth).transpose(1, 0, 2)
            blocks = lax.all_to_all(blocks, "grp", 0, 0, tiled=True)
            return gather_parts(blocks).transpose(1, 0, 2, 3).reshape(groups, -1, depth)

        input_columns = own_columns(
            lax.dynamic_slice_in_dim(gen_rows, own_start, local_rows, 0)
        )
        grad_columns = own_columns(branch_grad)

        hidden_near, hidden_far = gather_groups(gen_hidden)
        down_grad = None
        for piece, origin in zip(hidden_near + hidden_far, origins()):
            columns = lax.dynamic_index_in_dim(grad_columns, origin, 0, keepdims=False)
            term = dot(piece, columns, ((0,), (0,)))
            down_grad = term if down_grad is None else down_grad + term

        piece_grad = gather_parts(branch_grad).reshape(noise_all.shape)
        hidden_grad = None
        for piece, origin in zip(down_near + down_far, origins()):
            columns = lax.dynamic_slice_in_dim(piece_grad, origin * depth, depth, 1)
            term = dot(columns, piece, ((1,), (1,)))
            hidden_grad = term if hidden_grad is None else hidden_grad + term
        rows_grad = (hidden_grad * gate_slope(gen_pre)).astype(bf16)

        grad_near, grad_far = gather_groups(rows_grad)
        up_grad = None
        for piece, origin in zip(grad_near + grad_far, origins()):
            columns = lax.dynamic_index_in_dim(input_columns, origin, 0, keepdims=False)
            term = dot(columns, piece, ((0,), (0,)))
            up_grad = term if up_grad is None else up_grad + term
        return (generated[None], up_grad, down_grad)

    return per_device


def kernel_call(body, out_shapes, *operands, scalars=None, name, flops=0, moved=None):
    specs = [pl.BlockSpec(memory_space=pltpu.VMEM) for _ in operands]
    if scalars is not None:
        operands = (scalars, *operands)
        specs = [pl.BlockSpec(memory_space=pltpu.SMEM), *specs]
    total = sum(o.size * o.dtype.itemsize for o in operands)
    total += sum(o.size * jnp.dtype(o.dtype).itemsize for o in out_shapes)
    return pl.pallas_call(
        body,
        out_shape=tuple(out_shapes),
        in_specs=specs,
        out_specs=tuple(pl.BlockSpec(memory_space=pltpu.VMEM) for _ in out_shapes),
        compiler_params=pltpu.CompilerParams(vmem_limit_bytes=8 * 1024 * 1024),
        cost_estimate=pl.CostEstimate(flops=flops, bytes_accessed=total, transcendentals=0),
        name=name,
    )(*operands)


def settle(*arrays):
    def body(*refs):
        pass

    return pl.pallas_call(
        body,
        out_shape=tuple(jax.ShapeDtypeStruct(a.shape, a.dtype) for a in arrays),
        in_specs=[pl.BlockSpec(memory_space=pl.ANY) for _ in arrays],
        out_specs=tuple(pl.BlockSpec(memory_space=pl.ANY) for _ in arrays),
        input_output_aliases={i: i for i in range(len(arrays))},
        compiler_params=pltpu.CompilerParams(vmem_limit_bytes=256 * 1024),
        name="settle",
    )(*arrays)


def make_paired(groups, parts):
    pair, swap, far = 2, 1, 4
    core, side = 1, 2
    order = (0, side, core, core | side)
    masks = range(groups)

    def hop(values, axis, mask):
        size = groups if axis == "grp" else parts
        return lax.ppermute(values, axis, [(i, i ^ mask) for i in range(size)])

    def shape(*dims, dtype=bf16):
        return jax.ShapeDtypeStruct(dims, dtype)

    def gather_tokens(own):
        crossed = hop(own, "tp", side)
        return [own, crossed, hop(own, "tp", core), hop(crossed, "tp", core)]

    ring_pairs = [(g, (g + 2) % groups) for g in range(groups)]

    def ring(values):
        return lax.ppermute(values, "grp", ring_pairs)

    def send_blocks(blocks, mask):
        return hop(blocks[:, blocks.shape[1] // 2 :], "grp", mask)

    def with_arrived(blocks, arrived):
        return jnp.concatenate([blocks[:, : blocks.shape[1] // 2], arrived], 0)

    def own_columns(tokens, scalars):
        _, rows, depth = tokens[0].shape

        def body(s, *refs):
            for g in masks:
                for at, image_index in enumerate((g, g ^ pair)):
                    m = s[0] ^ image_index
                    spot = (m & pair) + (m & 1) * 4 + (m // 4)
                    for k, ref in enumerate(refs[:-1]):
                        start = (at * parts + k) * rows
                        refs[-1][g, start : start + rows, :] = ref[spot]

        (packed,) = kernel_call(
            body,
            [shape(groups, 2 * parts * rows, depth)],
            *tokens,
            scalars=scalars,
            name="pack",
        )
        return packed

    def per_device(
        gen_noise,
        diff_noise,
        timesteps,
        gen_mod,
        teacher_mod,
        critic_mod,
        gen_up,
        gen_down,
        teacher_up,
        teacher_down,
        critic_up,
        critic_down,
    ):
        rows = diff_noise.shape[1]
        image = gen_noise.shape[1]
        depth = gen_up.shape[0]
        width = gen_noise.shape[2]
        units = gen_up.shape[1] // 2
        middle = width // 2
        score_units = teacher_up.shape[1]
        level_count = teacher_mod.shape[0] + 1.0
        own = lax.axis_index("grp")
        part = lax.axis_index("tp")
        half = (own // pair) % 2
        scalars = jnp.stack([own, part, timesteps[0], half])

        def block(ref_own, m):
            return pl.ds(pl.multiple_of((ref_own ^ m) * depth, 128), depth)

        def fixed(m):
            return slice(m * depth, (m + 1) * depth)

        def halves(values, axis):
            return tuple(
                lax.dynamic_slice_in_dim(values, index * units, units, axis)
                for index in (half, 1 - half)
            )

        up, down = {}, {}
        up[0], up_send = halves(gen_up, 1)
        down[0], down_send = halves(gen_down, 0)

        def input_body(s, noise_ref, mod_ref, rows_ref, blocks_ref):
            for k, mask in enumerate(order):
                start = pl.multiple_of((s[1] ^ mask) * rows, 16)
                values = noise_ref[0, pl.ds(start, rows), :].astype(f32)
                values = normalize(values) * (1.0 + mod_ref[1:2]) + mod_ref[0:1]
                rows_ref[k * rows : (k + 1) * rows, :] = values.astype(bf16)
            for m in masks:
                blocks_ref[m] = rows_ref[:rows, block(s[0], m)]

        up[pair] = hop(up_send, "grp", pair)
        up[far] = hop(up[0], "grp", far)
        up[swap] = hop(up[0], "grp", swap)
        gen_rows, input_blocks = kernel_call(
            input_body,
            [shape(image, width), shape(groups, rows, depth)],
            gen_noise,
            gen_mod,
            scalars=scalars,
            name="input",
        )
        (
            up[pair],
            up[far],
            up[swap],
            down_send,
            gen_rows,
            input_blocks,
        ) = settle(up[pair], up[far], up[swap], down_send, gen_rows, input_blocks)
        up[pair | far] = hop(up[pair], "grp", far)
        up[pair | swap] = hop(up[pair], "grp", swap)
        up[far | swap] = hop(up[far], "grp", swap)
        down[pair] = hop(down_send, "grp", pair)
        pair_rows = gather_tokens(hop(gen_rows[:rows], "grp", pair))
        (
            up[pair | far],
            up[pair | swap],
            up[far | swap],
            down[pair],
            down[0],
        ) = settle(up[pair | far], up[pair | swap], up[far | swap], down[pair], down[0])
        up[pair | far | swap] = hop(up[pair | far], "grp", swap)
        down[far] = hop(down[0], "grp", far)
        down[swap] = hop(down[0], "grp", swap)
        up[pair | far | swap], down[pair], down[far], down[swap] = settle(
            up[pair | far | swap], down[pair], down[far], down[swap]
        )
        down[pair | far] = hop(down[pair], "grp", far)
        down[pair | swap] = hop(down[pair], "grp", swap)
        down[far | swap] = hop(down[far], "grp", swap)

        def pre_body(s, rows_ref, p0, p1, p2, p3, *refs):
            pieces, (pre_ref, hidden_ref) = refs[:groups], refs[groups:]
            for m in masks:
                spot = block(s[0], m)
                left = jnp.concatenate(
                    [rows_ref[:, spot]] + [p[:, spot] for p in (p0, p1, p2, p3)], 0
                )
                term = dot(left, pieces[m][...])
                if m == 0:
                    pre_ref[...] = term
                else:
                    pre_ref[...] += term
            hidden_ref[...] = smooth_gate(pre_ref[...]).astype(bf16)

        gen_pre, gen_hidden = kernel_call(
            pre_body,
            [shape(2 * image, units, dtype=f32), shape(2 * image, units)],
            gen_rows,
            *pair_rows,
            *[up[m] for m in masks],
            scalars=scalars,
            name="pre",
            flops=4 * image * width * units,
        )

        def branch_body(hidden_ref, *refs):
            pieces, (keep_ref, send_ref) = refs[:-2], refs[-2:]
            for m, piece in enumerate(pieces):
                for image_at, spot in ((0, m), (1, m ^ pair)):
                    values = dot(
                        hidden_ref[image_at * image : (image_at + 1) * image, :], piece[...]
                    )
                    cut = slice(image_at * image // 2, (image_at + 1) * image // 2)
                    keep_ref[cut, fixed(spot)] = values[: image // 2]
                    send_ref[cut, fixed(spot)] = values[image // 2 :].astype(bf16)

        def core_body(keep_ref, got_ref, first_ref, second_ref, third_ref, rest_ref):
            def total(at):
                cut = slice(at * rows, (at + 1) * rows)
                return keep_ref[cut, :] + got_ref[cut, :].astype(f32)

            first_ref[...] = total(3).astype(bf16)
            second_ref[...] = total(1).astype(bf16)
            third_ref[...] = total(2)
            rest_ref[...] = total(0)

        def add_body(left_ref, right_ref, out_ref):
            out_ref[...] = (left_ref[...] + right_ref[...].astype(f32)).astype(bf16)

        def branch_core(which, hidden):
            count = groups // 2
            keep, send = kernel_call(
                branch_body,
                [shape(image, middle, dtype=f32), shape(image, middle)],
                hidden,
                *[down[m] for m in masks if m // count == which],
                name="branch",
                flops=2 * image * width * units,
            )
            return kernel_call(
                core_body,
                [shape(rows, middle)] * 2 + [shape(rows, middle, dtype=f32)] * 2,
                keep,
                hop(send, "tp", core),
                name="core_sum",
            )

        def branch_sum(first, second, third, rest):
            (third,) = kernel_call(
                add_body,
                [shape(rows, middle)],
                third,
                hop(first, "tp", side),
                name="side_sum",
            )
            return rest, hop(second, "tp", side), hop(third, "grp", pair)

        (
            down[pair | far],
            down[pair | swap],
            down[far | swap],
            gen_hidden,
            input_blocks,
        ) = settle(
            down[pair | far],
            down[pair | swap],
            down[far | swap],
            gen_hidden,
            input_blocks[None],
        )
        down[pair | far | swap] = hop(down[pair | far], "grp", swap)
        arrived = send_blocks(input_blocks, far)
        left_terms = branch_core(0, gen_hidden)
        down[pair | far | swap], gen_hidden, arrived, *left_terms = settle(
            down[pair | far | swap], gen_hidden, arrived, *left_terms
        )
        left_sum = branch_sum(*left_terms)
        hidden_near = [gen_hidden, ring(gen_hidden)]
        hidden_across = [hop(gen_hidden, "grp", swap)]
        input_blocks = with_arrived(input_blocks, arrived)
        arrived = send_blocks(input_blocks, pair)
        right_sum = branch_sum(*branch_core(1, gen_hidden))

        def latent_body(s, noise_ref, diff_ref, mod_ref, *refs):
            sums, (generated_ref, noised_ref) = refs[:6], refs[6:]
            level = (s[2].astype(f32) + 1.0) / level_count
            start = pl.multiple_of(s[1] * rows, 16)
            for m in masks:
                which, at = divmod(m, groups // 2)
                a, b, c = sums[3 * which : 3 * which + 3]
                branch = (
                    a[:, fixed(at)] + b[:, fixed(at)].astype(f32) + c[:, fixed(at)].astype(f32)
                )
                spot = block(s[0], m)
                noise = noise_ref[0, pl.ds(start, rows), spot].astype(f32)
                made = (noise + mod_ref[2:3, spot] * branch).astype(bf16)
                generated_ref[0, :, spot] = made
                noised_ref[:, spot] = (
                    (1.0 - level) * made.astype(f32) + level * diff_ref[0, :, spot].astype(f32)
                ).astype(bf16)

        generated, noised = kernel_call(
            latent_body,
            [shape(1, rows, width), shape(rows, width)],
            gen_noise,
            diff_noise,
            gen_mod,
            *left_sum,
            *right_sum,
            scalars=scalars,
            name="latent",
        )

        noised, hidden_near[1], hidden_across[0], arrived = settle(
            noised, hidden_near[1], hidden_across[0], arrived
        )
        hidden_near.append(ring(hidden_near[1]))
        hidden_across.append(hop(hidden_near[1], "grp", swap))
        input_blocks = with_arrived(input_blocks, arrived)
        arrived = send_blocks(input_blocks, swap)

        def score_input_body(s, n0, n1, n2, n3, teacher_ref, critic_ref, t_ref, c_ref):
            for k, part_ref in enumerate((n0, n1, n2, n3)):
                normed = normalize(part_ref[...].astype(f32))
                cut = slice(k * rows, (k + 1) * rows)
                for table, out in ((teacher_ref, t_ref), (critic_ref, c_ref)):
                    row = table[s[2]]
                    out[cut, :] = (normed * (1.0 + row[1:2]) + row[0:1]).astype(bf16)

        teacher_in, critic_in = kernel_call(
            score_input_body,
            [shape(image, width)] * 2,
            *gather_tokens(noised),
            teacher_mod,
            critic_mod,
            scalars=scalars,
            name="score_input",
        )


        tile = 256

        def hidden_body(t_in, c_in, t_w, c_w, t_out, c_out):
            t_out[...] = smooth_gate(dot(t_in[...], t_w[...])).astype(bf16)
            c_out[...] = smooth_gate(dot(c_in[...], c_w[...])).astype(bf16)

        whole = pl.BlockSpec((image, width), lambda j: (0, 0))
        teacher_hidden, critic_hidden = pl.pallas_call(
            hidden_body,
            grid=(score_units // tile,),
            in_specs=[whole, whole] + [pl.BlockSpec((width, tile), lambda j: (0, j))] * 2,
            out_specs=[pl.BlockSpec((image, tile), lambda j: (0, j))] * 2,
            out_shape=[shape(image, score_units)] * 2,
            compiler_params=pltpu.CompilerParams(vmem_limit_bytes=8 * 1024 * 1024),
            cost_estimate=pl.CostEstimate(
                flops=4 * image * width * score_units,
                bytes_accessed=4 * width * score_units,
                transcendentals=0,
            ),
            name="score_hidden",
        )(teacher_in, critic_in, teacher_up, critic_up)

        teacher_hidden, hidden_near[2], hidden_across[1], arrived = settle(
            teacher_hidden, hidden_near[2], hidden_across[1], arrived
        )
        hidden_near.append(ring(hidden_near[2]))
        hidden_across.append(hop(hidden_near[2], "grp", swap))
        input_tokens = [with_arrived(input_blocks, arrived)[:, 0]]
        input_tokens.append(hop(input_tokens[0], "tp", side))

        def gap_body(s, t_h, c_h, t_w, c_w, t_mod, c_mod, keep_ref, send_ref):
            values = t_mod[s[2], 2:3] * dot(t_h[...], t_w[...]) - c_mod[s[2], 2:3] * dot(
                c_h[...], c_w[...]
            )
            keep_ref[...] = values[: image // 2]
            send_ref[...] = values[image // 2 :].astype(bf16)

        whole = pl.BlockSpec((image, score_units), lambda j: (0, 0))
        keep, send = pl.pallas_call(
            gap_body,
            grid=(width // tile,),
            in_specs=[pl.BlockSpec(memory_space=pltpu.SMEM), whole, whole]
            + [pl.BlockSpec((score_units, tile), lambda j: (0, j))] * 2
            + [pl.BlockSpec((*teacher_mod.shape[:2], tile), lambda j: (0, 0, j))] * 2,
            out_specs=[pl.BlockSpec((image // 2, tile), lambda j: (0, j))] * 2,
            out_shape=[shape(image // 2, width, dtype=f32), shape(image // 2, width)],
            compiler_params=pltpu.CompilerParams(vmem_limit_bytes=8 * 1024 * 1024),
            cost_estimate=pl.CostEstimate(
                flops=4 * image * width * score_units,
                bytes_accessed=4 * width * score_units,
                transcendentals=0,
            ),
            name="score_gap",
        )(scalars, teacher_hidden, critic_hidden, teacher_down, critic_down, teacher_mod, critic_mod)

        send, *input_tokens = settle(send, *input_tokens)
        input_tokens += [hop(values, "tp", core) for values in input_tokens]

        def gap_core_body(keep_ref, got_ref, send_ref, rest_ref):
            send_ref[...] = (keep_ref[rows:, :] + got_ref[rows:, :].astype(f32)).astype(bf16)
            rest_ref[...] = keep_ref[:rows, :] + got_ref[:rows, :].astype(f32)

        send, rest = kernel_call(
            gap_core_body,
            [shape(rows, width), shape(rows, width, dtype=f32)],
            keep,
            hop(send, "tp", core),
            name="gap_core",
        )

        def grad_body(s, rest_ref, got_ref, mod_ref, rows_ref, blocks_ref):
            level = (s[2].astype(f32) + 1.0) / level_count
            for m in masks:
                spot = block(s[0], m)
                gap = level * (rest_ref[:, spot] + got_ref[:, spot].astype(f32))
                values = (mod_ref[2:3, spot] * gap).astype(bf16)
                rows_ref[:, fixed(m)] = values
                blocks_ref[m] = values

        branch_grad, grad_blocks = kernel_call(
            grad_body,
            [shape(rows, width), shape(groups, rows, depth)],
            rest,
            hop(send, "tp", side),
            gen_mod,
            scalars=scalars,
            name="branch_grad",
        )

        branch_grad, grad_blocks, hidden_near[3], hidden_across[2] = settle(
            branch_grad, grad_blocks[None], hidden_near[3], hidden_across[2]
        )
        hidden_across.append(hop(hidden_near[3], "grp", swap))
        pair_grad = hop(branch_grad, "grp", pair)
        crossed = hop(branch_grad, "tp", side)
        arrived = send_blocks(grad_blocks, far)
        pair_grad, crossed, arrived = settle(pair_grad, crossed, arrived)
        pair_crossed = hop(pair_grad, "tp", side)
        own_tokens = [branch_grad, crossed]
        own_tokens += [hop(values, "tp", core) for values in own_tokens]
        grad_blocks = with_arrived(grad_blocks, arrived)
        arrived = send_blocks(grad_blocks, pair)
        pair_core = hop(pair_grad, "tp", core)
        pair_crossed, arrived = settle(pair_crossed, arrived)
        pair_tokens = [pair_grad, pair_crossed, pair_core, hop(pair_crossed, "tp", core)]

        def rows_grad_body(*refs):
            tokens, pieces = refs[:8], refs[8 : 8 + groups]
            pre_ref, out_ref, total = refs[8 + groups :]
            for m in masks:
                left = jnp.concatenate(
                    [t[:, fixed(m)] for t in tokens[:4]]
                    + [t[:, fixed(m ^ pair)] for t in tokens[4:]],
                    0,
                )
                term = dot(left, pieces[m][...], ((1,), (1,)))
                if m == 0:
                    total[...] = term
                else:
                    total[...] += term
            out_ref[...] = (total[...] * gate_slope(pre_ref[...])).astype(bf16)

        operands = (*own_tokens, *pair_tokens, *[down[m] for m in masks], gen_pre)
        rows_grad = pl.pallas_call(
            rows_grad_body,
            out_shape=shape(2 * image, units),
            in_specs=[pl.BlockSpec(memory_space=pltpu.VMEM) for _ in operands],
            out_specs=pl.BlockSpec(memory_space=pltpu.VMEM),
            scratch_shapes=[pltpu.VMEM((2 * image, units), f32)],
            compiler_params=pltpu.CompilerParams(vmem_limit_bytes=8 * 1024 * 1024),
            cost_estimate=pl.CostEstimate(
                flops=4 * image * width * units, bytes_accessed=10**7, transcendentals=0
            ),
            name="rows_grad",
        )(*operands)

        rows_grad, arrived, hidden_across[3] = settle(rows_grad, arrived, hidden_across[3])
        near, across = [rows_grad, ring(rows_grad)], [hop(rows_grad, "grp", swap)]
        grad_blocks = with_arrived(grad_blocks, arrived)
        arrived = send_blocks(grad_blocks, swap)
        near[1], across[0], arrived = settle(near[1], across[0], arrived)
        near.append(ring(near[1]))
        across.append(hop(near[1], "grp", swap))
        grad_tokens = gather_tokens(with_arrived(grad_blocks, arrived)[:, 0])
        near[2], across[1], *grad_tokens = settle(near[2], across[1], *grad_tokens)
        near.append(ring(near[2]))
        across.append(hop(near[2], "grp", swap))
        input_columns = own_columns(input_tokens, scalars)
        grad_columns = own_columns(grad_tokens, scalars)

        def columns_at(table, k, other):
            origin = lax.rem(own + groups - 2 * k, groups) ^ other
            return lax.dynamic_index_in_dim(table, origin, 0, keepdims=False)

        def in_order(table, near, across, last=()):
            for k, piece in enumerate(near):
                yield k % 2, columns_at(table, k, 0), piece
            for k, piece in enumerate(across):
                yield k % 2, columns_at(table, k, swap), piece
            for at, piece in enumerate(last):
                columns = columns_at(table, groups // 2 - 1, swap)
                yield 1, columns[at * image : (at + 1) * image], piece

        def over_tokens(left, right):
            return dot(left, right, ((0,), (0,)))

        def join_halves(mine, other, axis):
            return jnp.where(
                half == 0,
                jnp.concatenate([mine, other], axis),
                jnp.concatenate([other, mine], axis),
            )

        down_sums = [0.0, 0.0]
        for which, columns, piece in in_order(
            grad_columns, hidden_near, hidden_across
        ):
            down_sums[which] += over_tokens(piece, columns)
        near[-1], across[-1], *down_sums = settle(near[-1], across[-1], *down_sums)
        last = [hop(near[-1][:image], "grp", swap), ring(across[-1][image:])]
        up_sums = [0.0, 0.0]
        for which, columns, piece in in_order(input_columns, near, across, last):
            up_sums[which] += over_tokens(columns, piece)
        return generated, join_halves(*up_sums, 1), join_halves(*down_sums, 0)

    return per_device


def make_per_device(groups, parts):
    def per_device(*args):
        depth, units = args[6].shape
        fits = depth % 128 == 0 and units % 512 == 0 and args[1].shape[1] % 16 == 0
        if groups == 8 and parts == 4 and fits:
            return make_paired(groups, parts)(*args)
        return make_ring(groups, parts)(*args)

    return per_device


def solution(mesh):
    in_specs = (
        P("grp", None, None),
        P("grp", "tp", None),
        P("grp"),
        P(),
        P(),
        P(),
        P("grp", "tp"),
        P("tp", "grp"),
        P(None, "tp"),
        P("tp", None),
        P(None, "tp"),
        P("tp", None),
    )
    out_specs = (P("grp", "tp", None), P("grp", "tp"), P("tp", "grp"))
    return jax.shard_map(
        make_per_device(mesh.shape["grp"], mesh.shape["tp"]),
        mesh=mesh,
        in_specs=in_specs,
        out_specs=out_specs,
        check_vma=False,
    )
```

```python
import jax
import jax.numpy as jnp
from jax import lax
from jax.experimental import pallas as pl
from jax.experimental.pallas import tpu as pltpu
from jax.sharding import PartitionSpec as P

epsilon = 1e-06
root_two_pi = 0.7978845608028654
cubic = 0.044715
f32 = jnp.float32
bf16 = jnp.bfloat16


def normalize(values):
    center = values - jnp.mean(values, axis=-1, keepdims=True)
    spread = jnp.mean(center * center, axis=-1, keepdims=True)
    return center * lax.rsqrt(spread + epsilon)


def smooth_gate(values):
    inner = root_two_pi * (values + cubic * values * values * values)
    return 0.5 * values * (1.0 + jnp.tanh(inner))


def gate_slope(values):
    inner = root_two_pi * (values + cubic * values * values * values)
    tangent = jnp.tanh(inner)
    return 0.5 * (1.0 + tangent) + 0.5 * values * (1.0 - tangent * tangent) * root_two_pi * (
        1.0 + 3.0 * cubic * values * values
    )


def pick_level(table, step_index):
    levels = lax.broadcasted_iota(jnp.int32, (table.shape[0], 1, 1), 0)
    return jnp.sum(jnp.where(levels == step_index, table, 0.0), axis=0)


def modulate(normed, picked):
    return (normed * (1.0 + picked[1]) + picked[0]).astype(bf16)


def dot(left, right, contract=((1,), (0,))):
    return lax.dot_general(left, right, (contract, ((), ())), preferred_element_type=f32)


def make_ring(groups, parts):
    places = groups // 2
    ring_pairs = [(2 * p + s, 2 * ((p + 1) % places) + s) for p in range(places) for s in range(2)]
    swap_pairs = [(g, g ^ 1) for g in range(groups)]

    def ring(piece):
        return lax.ppermute(piece, "grp", ring_pairs)

    def swap(piece):
        return lax.ppermute(piece, "grp", swap_pairs)

    def gather_groups(own):
        near, far = [own], []
        for _ in range(places - 1):
            far.append(swap(near[-1]))
            near.append(ring(near[-1]))
        half = own.shape[0] // 2
        first = swap(near[-1][:half])
        second = ring(far[-1][half:]) if far else swap(near[-1][half:])
        far.append(jnp.concatenate([first, second], axis=0))
        return near, far

    def bit_pairs(bit):
        return [(t, t ^ (1 << bit)) for t in range(parts)]

    bits = parts.bit_length() - 1

    def sum_parts(values):
        place = lax.axis_index("tp")
        blocks = values.reshape(parts, values.shape[0] // parts, values.shape[1])
        for bit in range(bits):
            mine = (place >> bit) & 1
            split = blocks.reshape(blocks.shape[0] // 2, 2, *blocks.shape[1:])
            keep = lax.dynamic_index_in_dim(split, mine, 1, keepdims=False)
            send = lax.dynamic_index_in_dim(split, 1 - mine, 1, keepdims=False)
            if bit > 0:
                send = send.astype(bf16)
            blocks = keep + lax.ppermute(send, "tp", bit_pairs(bit)).astype(f32)
        return blocks[0]

    def gather_parts(values):
        place = lax.axis_index("tp")
        blocks = values[None]
        for bit in reversed(range(bits)):
            mine = (place >> bit) & 1
            other = lax.ppermute(blocks, "tp", bit_pairs(bit))
            pair = jnp.where(
                mine == 0, jnp.stack([blocks, other], 1), jnp.stack([other, blocks], 1)
            )
            blocks = pair.reshape(-1, *values.shape)
        return blocks

    def per_device(
        gen_noise,
        diff_noise,
        timesteps,
        gen_mod,
        teacher_mod,
        critic_mod,
        gen_up,
        gen_down,
        teacher_up,
        teacher_down,
        critic_up,
        critic_down,
    ):
        local_rows = diff_noise.shape[1]
        depth = gen_up.shape[0]
        step_index = timesteps[0]
        own = lax.axis_index("grp")
        place, side = own // 2, own % 2
        own_start = lax.axis_index("tp") * local_rows

        def origins():
            for k in range(places):
                yield lax.rem(place - k + places, places) * 2 + side
            for k in range(places):
                yield lax.rem(place - k + places, places) * 2 + 1 - side

        def to_absolute(near, far):
            order = [(-r) % places for r in range(places)]
            pairs = [
                jnp.where(
                    side == 0,
                    jnp.concatenate([near[k], far[k]], 1),
                    jnp.concatenate([far[k], near[k]], 1),
                )
                for k in order
            ]
            both = jnp.concatenate(pairs + pairs[:-1], 1)
            width = pairs[0].shape[1]
            start = lax.rem(places - place, places) * width
            return lax.dynamic_slice_in_dim(both, start, width * places, 1)

        noise_all = gen_noise[0].astype(f32)
        gen_rows = modulate(normalize(noise_all), gen_mod)
        noise = lax.dynamic_slice_in_dim(noise_all, own_start, local_rows, 0)

        up_near, up_far = gather_groups(gen_up)
        down_near, down_far = gather_groups(gen_down)

        gen_pre = None
        for piece, origin in zip(up_near + up_far, origins()):
            term = dot(lax.dynamic_slice_in_dim(gen_rows, origin * depth, depth, 1), piece)
            gen_pre = term if gen_pre is None else gen_pre + term
        gen_hidden = smooth_gate(gen_pre).astype(bf16)

        branch_near = [dot(gen_hidden, piece) for piece in down_near]
        branch_far = [dot(gen_hidden, piece) for piece in down_far]
        partial = to_absolute(branch_near, branch_far)
        gen_branch = sum_parts(partial)

        generated = (noise + gen_mod[2] * gen_branch).astype(bf16)
        level = (step_index.astype(f32) + 1.0) / (teacher_mod.shape[0] + 1)
        noised = (
            (1.0 - level) * generated.astype(f32) + level * diff_noise[0].astype(f32)
        ).astype(bf16)
        teacher_row = pick_level(teacher_mod, step_index)
        critic_row = pick_level(critic_mod, step_index)
        noised_all = gather_parts(lax.optimization_barrier(noised)).reshape(
            noise_all.shape
        )
        normed = normalize(noised_all.astype(f32))

        def score(row, weight_up, weight_down):
            hidden = smooth_gate(dot(modulate(normed, row), weight_up)).astype(bf16)
            return row[2] * dot(hidden, weight_down)

        gap_part = score(teacher_row, teacher_up, teacher_down) - score(
            critic_row, critic_up, critic_down
        )
        gap = level * sum_parts(gap_part)
        branch_grad = (gen_mod[2] * gap).astype(bf16)

        def own_columns(rows):
            count = rows.shape[0]
            blocks = rows.reshape(count, groups, depth).transpose(1, 0, 2)
            blocks = lax.all_to_all(blocks, "grp", 0, 0, tiled=True)
            return gather_parts(blocks).transpose(1, 0, 2, 3).reshape(groups, -1, depth)

        input_columns = own_columns(
            lax.dynamic_slice_in_dim(gen_rows, own_start, local_rows, 0)
        )
        grad_columns = own_columns(branch_grad)

        hidden_near, hidden_far = gather_groups(gen_hidden)
        down_grad = None
        for piece, origin in zip(hidden_near + hidden_far, origins()):
            columns = lax.dynamic_index_in_dim(grad_columns, origin, 0, keepdims=False)
            term = dot(piece, columns, ((0,), (0,)))
            down_grad = term if down_grad is None else down_grad + term

        piece_grad = gather_parts(branch_grad).reshape(noise_all.shape)
        hidden_grad = None
        for piece, origin in zip(down_near + down_far, origins()):
            columns = lax.dynamic_slice_in_dim(piece_grad, origin * depth, depth, 1)
            term = dot(columns, piece, ((1,), (1,)))
            hidden_grad = term if hidden_grad is None else hidden_grad + term
        rows_grad = (hidden_grad * gate_slope(gen_pre)).astype(bf16)

        grad_near, grad_far = gather_groups(rows_grad)
        up_grad = None
        for piece, origin in zip(grad_near + grad_far, origins()):
            columns = lax.dynamic_index_in_dim(input_columns, origin, 0, keepdims=False)
            term = dot(columns, piece, ((0,), (0,)))
            up_grad = term if up_grad is None else up_grad + term
        return (generated[None], up_grad, down_grad)

    return per_device


def kernel_call(body, out_shapes, *operands, scalars=None, name, flops=0, moved=None):
    specs = [pl.BlockSpec(memory_space=pltpu.VMEM) for _ in operands]
    if scalars is not None:
        operands = (scalars, *operands)
        specs = [pl.BlockSpec(memory_space=pltpu.SMEM), *specs]
    total = sum(o.size * o.dtype.itemsize for o in operands)
    total += sum(o.size * jnp.dtype(o.dtype).itemsize for o in out_shapes)
    return pl.pallas_call(
        body,
        out_shape=tuple(out_shapes),
        in_specs=specs,
        out_specs=tuple(pl.BlockSpec(memory_space=pltpu.VMEM) for _ in out_shapes),
        compiler_params=pltpu.CompilerParams(vmem_limit_bytes=8 * 1024 * 1024),
        cost_estimate=pl.CostEstimate(flops=flops, bytes_accessed=total, transcendentals=0),
        name=name,
    )(*operands)


def settle(*arrays):
    def body(*refs):
        pass

    return pl.pallas_call(
        body,
        out_shape=tuple(jax.ShapeDtypeStruct(a.shape, a.dtype) for a in arrays),
        in_specs=[pl.BlockSpec(memory_space=pl.ANY) for _ in arrays],
        out_specs=tuple(pl.BlockSpec(memory_space=pl.ANY) for _ in arrays),
        input_output_aliases={i: i for i in range(len(arrays))},
        compiler_params=pltpu.CompilerParams(vmem_limit_bytes=256 * 1024),
        name="settle",
    )(*arrays)


def make_paired(groups, parts):
    pair, swap, far = 2, 1, 4
    core, side = 1, 2
    order = (0, side, core, core | side)
    masks = range(groups)

    def hop(values, axis, mask):
        size = groups if axis == "grp" else parts
        return lax.ppermute(values, axis, [(i, i ^ mask) for i in range(size)])

    def shape(*dims, dtype=bf16):
        return jax.ShapeDtypeStruct(dims, dtype)

    def gather_tokens(own):
        crossed = hop(own, "tp", side)
        return [own, crossed, hop(own, "tp", core), hop(crossed, "tp", core)]

    ring_pairs = [(g, (g + 2) % groups) for g in range(groups)]

    def ring(values):
        return lax.ppermute(values, "grp", ring_pairs)

    def send_blocks(blocks, mask):
        return hop(blocks[:, blocks.shape[1] // 2 :], "grp", mask)

    def with_arrived(blocks, arrived):
        return jnp.concatenate([blocks[:, : blocks.shape[1] // 2], arrived], 0)

    def own_columns(tokens, scalars, sent):
        _, rows, depth = tokens[0].shape

        def body(s, *refs):
            for g in masks:
                for at, image_index in enumerate((g, g ^ pair)):
                    m = s[0] ^ image_index
                    spot = sum(((m // bit) & 1) << place for place, bit in enumerate(sent))
                    for k, ref in enumerate(refs[:-1]):
                        start = (at * parts + k) * rows
                        refs[-1][g, start : start + rows, :] = ref[spot]

        (packed,) = kernel_call(
            body,
            [shape(groups, 2 * parts * rows, depth)],
            *tokens,
            scalars=scalars,
            name="pack",
        )
        return packed

    def per_device(
        gen_noise,
        diff_noise,
        timesteps,
        gen_mod,
        teacher_mod,
        critic_mod,
        gen_up,
        gen_down,
        teacher_up,
        teacher_down,
        critic_up,
        critic_down,
    ):
        rows = diff_noise.shape[1]
        image = gen_noise.shape[1]
        depth = gen_up.shape[0]
        width = gen_noise.shape[2]
        units = gen_up.shape[1] // 2
        middle = width // 2
        score_units = teacher_up.shape[1]
        level_count = teacher_mod.shape[0] + 1.0
        own = lax.axis_index("grp")
        part = lax.axis_index("tp")
        half = (own // pair) % 2
        scalars = jnp.stack([own, part, timesteps[0], half])

        def block(ref_own, m):
            return pl.ds(pl.multiple_of((ref_own ^ m) * depth, 128), depth)

        def fixed(m):
            return slice(m * depth, (m + 1) * depth)

        def halves(values, axis):
            return tuple(
                lax.dynamic_slice_in_dim(values, index * units, units, axis)
                for index in (half, 1 - half)
            )

        up, down = {}, {}
        up[0], up_send = halves(gen_up, 1)
        down[0], down_send = halves(gen_down, 0)

        def input_body(s, noise_ref, mod_ref, rows_ref, blocks_ref):
            for k, mask in enumerate(order):
                start = pl.multiple_of((s[1] ^ mask) * rows, 16)
                values = noise_ref[0, pl.ds(start, rows), :].astype(f32)
                values = normalize(values) * (1.0 + mod_ref[1:2]) + mod_ref[0:1]
                rows_ref[k * rows : (k + 1) * rows, :] = values.astype(bf16)
            for m in masks:
                place = (m & pair) * 2 + (m & far) // 2 + (m & swap)
                blocks_ref[place] = rows_ref[:rows, block(s[0], m)]

        up[pair] = hop(up_send, "grp", pair)
        up[far] = hop(up[0], "grp", far)
        up[swap] = hop(up[0], "grp", swap)
        gen_rows, input_blocks = kernel_call(
            input_body,
            [shape(image, width), shape(groups, rows, depth)],
            gen_noise,
            gen_mod,
            scalars=scalars,
            name="input",
        )
        (
            up[pair],
            up[far],
            up[swap],
            down_send,
            gen_rows,
            input_blocks,
        ) = settle(up[pair], up[far], up[swap], down_send, gen_rows, input_blocks)
        up[pair | far] = hop(up[pair], "grp", far)
        up[pair | swap] = hop(up[pair], "grp", swap)
        up[far | swap] = hop(up[far], "grp", swap)
        down[pair] = hop(down_send, "grp", pair)
        pair_rows = gather_tokens(hop(gen_rows[:rows], "grp", pair))
        (
            up[pair | far],
            up[pair | swap],
            up[far | swap],
            down[pair],
            down[0],
        ) = settle(up[pair | far], up[pair | swap], up[far | swap], down[pair], down[0])
        up[pair | far | swap] = hop(up[pair | far], "grp", swap)
        down[far] = hop(down[0], "grp", far)
        down[swap] = hop(down[0], "grp", swap)
        up[pair | far | swap], down[pair], down[far], down[swap], input_blocks = settle(
            up[pair | far | swap], down[pair], down[far], down[swap], input_blocks[None]
        )
        arrived = send_blocks(input_blocks, pair)
        down[pair | far] = hop(down[pair], "grp", far)
        down[pair | swap] = hop(down[pair], "grp", swap)
        down[far | swap] = hop(down[far], "grp", swap)

        def pre_body(s, rows_ref, p0, p1, p2, p3, *refs):
            pieces, (pre_ref, hidden_ref) = refs[:groups], refs[groups:]
            for m in masks:
                spot = block(s[0], m)
                left = jnp.concatenate(
                    [rows_ref[:, spot]] + [p[:, spot] for p in (p0, p1, p2, p3)], 0
                )
                term = dot(left, pieces[m][...])
                if m == 0:
                    pre_ref[...] = term
                else:
                    pre_ref[...] += term
            hidden_ref[...] = smooth_gate(pre_ref[...]).astype(bf16)

        gen_pre, gen_hidden = kernel_call(
            pre_body,
            [shape(2 * image, units, dtype=f32), shape(2 * image, units)],
            gen_rows,
            *pair_rows,
            *[up[m] for m in masks],
            scalars=scalars,
            name="pre",
            flops=4 * image * width * units,
        )

        def branch_body(hidden_ref, *refs):
            pieces, (keep_ref, send_ref) = refs[:-2], refs[-2:]
            for m, piece in enumerate(pieces):
                for image_at, spot in ((0, m), (1, m ^ pair)):
                    values = dot(
                        hidden_ref[image_at * image : (image_at + 1) * image, :], piece[...]
                    )
                    cut = slice(image_at * image // 2, (image_at + 1) * image // 2)
                    keep_ref[cut, fixed(spot)] = values[: image // 2]
                    send_ref[cut, fixed(spot)] = values[image // 2 :].astype(bf16)

        def core_body(keep_ref, got_ref, first_ref, second_ref, third_ref, rest_ref):
            def total(at):
                cut = slice(at * rows, (at + 1) * rows)
                return keep_ref[cut, :] + got_ref[cut, :].astype(f32)

            first_ref[...] = total(3).astype(bf16)
            second_ref[...] = total(1).astype(bf16)
            third_ref[...] = total(2)
            rest_ref[...] = total(0)

        def add_body(left_ref, right_ref, out_ref):
            out_ref[...] = (left_ref[...] + right_ref[...].astype(f32)).astype(bf16)

        def branch_core(which, hidden):
            count = groups // 2
            keep, send = kernel_call(
                branch_body,
                [shape(image, middle, dtype=f32), shape(image, middle)],
                hidden,
                *[down[m] for m in masks if m // count == which],
                name="branch",
                flops=2 * image * width * units,
            )
            return kernel_call(
                core_body,
                [shape(rows, middle)] * 2 + [shape(rows, middle, dtype=f32)] * 2,
                keep,
                hop(send, "tp", core),
                name="core_sum",
            )

        def branch_sum(first, second, third, rest):
            (third,) = kernel_call(
                add_body,
                [shape(rows, middle)],
                third,
                hop(first, "tp", side),
                name="side_sum",
            )
            return rest, hop(second, "tp", side), hop(third, "grp", pair)

        (
            down[pair | far],
            down[pair | swap],
            down[far | swap],
            gen_hidden,
            arrived,
        ) = settle(
            down[pair | far],
            down[pair | swap],
            down[far | swap],
            gen_hidden,
            arrived,
        )
        input_blocks = with_arrived(input_blocks, arrived)
        down[pair | far | swap] = hop(down[pair | far], "grp", swap)
        arrived = send_blocks(input_blocks, far)
        left_terms = branch_core(0, gen_hidden)
        down[pair | far | swap], gen_hidden, arrived, *left_terms = settle(
            down[pair | far | swap], gen_hidden, arrived, *left_terms
        )
        left_sum = branch_sum(*left_terms)
        hidden_near = [gen_hidden, ring(gen_hidden)]
        hidden_across = [hop(gen_hidden, "grp", swap)]
        right_sum = branch_sum(*branch_core(1, gen_hidden))

        def latent_body(s, noise_ref, diff_ref, mod_ref, *refs):
            sums, (generated_ref, noised_ref) = refs[:6], refs[6:]
            level = (s[2].astype(f32) + 1.0) / level_count
            start = pl.multiple_of(s[1] * rows, 16)
            for m in masks:
                which, at = divmod(m, groups // 2)
                a, b, c = sums[3 * which : 3 * which + 3]
                branch = (
                    a[:, fixed(at)] + b[:, fixed(at)].astype(f32) + c[:, fixed(at)].astype(f32)
                )
                spot = block(s[0], m)
                noise = noise_ref[0, pl.ds(start, rows), spot].astype(f32)
                made = (noise + mod_ref[2:3, spot] * branch).astype(bf16)
                generated_ref[0, :, spot] = made
                noised_ref[:, spot] = (
                    (1.0 - level) * made.astype(f32) + level * diff_ref[0, :, spot].astype(f32)
                ).astype(bf16)

        generated, noised = kernel_call(
            latent_body,
            [shape(1, rows, width), shape(rows, width)],
            gen_noise,
            diff_noise,
            gen_mod,
            *left_sum,
            *right_sum,
            scalars=scalars,
            name="latent",
        )

        noised, hidden_near[1], hidden_across[0], arrived = settle(
            noised, hidden_near[1], hidden_across[0], arrived
        )
        hidden_near.append(ring(hidden_near[1]))
        hidden_across.append(hop(hidden_near[1], "grp", swap))
        input_blocks = with_arrived(input_blocks, arrived)
        arrived = send_blocks(input_blocks, swap)

        def score_input_body(s, n0, n1, n2, n3, teacher_ref, critic_ref, t_ref, c_ref):
            for k, part_ref in enumerate((n0, n1, n2, n3)):
                normed = normalize(part_ref[...].astype(f32))
                cut = slice(k * rows, (k + 1) * rows)
                for table, out in ((teacher_ref, t_ref), (critic_ref, c_ref)):
                    row = table[s[2]]
                    out[cut, :] = (normed * (1.0 + row[1:2]) + row[0:1]).astype(bf16)

        teacher_in, critic_in = kernel_call(
            score_input_body,
            [shape(image, width)] * 2,
            *gather_tokens(noised),
            teacher_mod,
            critic_mod,
            scalars=scalars,
            name="score_input",
        )


        tile = 256

        def hidden_body(t_in, c_in, t_w, c_w, t_out, c_out):
            t_out[...] = smooth_gate(dot(t_in[...], t_w[...])).astype(bf16)
            c_out[...] = smooth_gate(dot(c_in[...], c_w[...])).astype(bf16)

        whole = pl.BlockSpec((image, width), lambda j: (0, 0))
        teacher_hidden, critic_hidden = pl.pallas_call(
            hidden_body,
            grid=(score_units // tile,),
            in_specs=[whole, whole] + [pl.BlockSpec((width, tile), lambda j: (0, j))] * 2,
            out_specs=[pl.BlockSpec((image, tile), lambda j: (0, j))] * 2,
            out_shape=[shape(image, score_units)] * 2,
            compiler_params=pltpu.CompilerParams(vmem_limit_bytes=8 * 1024 * 1024),
            cost_estimate=pl.CostEstimate(
                flops=4 * image * width * score_units,
                bytes_accessed=4 * width * score_units,
                transcendentals=0,
            ),
            name="score_hidden",
        )(teacher_in, critic_in, teacher_up, critic_up)

        teacher_hidden, hidden_near[2], hidden_across[1], arrived = settle(
            teacher_hidden, hidden_near[2], hidden_across[1], arrived
        )
        hidden_near.append(ring(hidden_near[2]))
        hidden_across.append(hop(hidden_near[2], "grp", swap))
        input_tokens = [with_arrived(input_blocks, arrived)[:, 0]]
        input_tokens.append(hop(input_tokens[0], "tp", side))

        def gap_body(s, t_h, c_h, t_w, c_w, t_mod, c_mod, keep_ref, send_ref):
            values = t_mod[s[2], 2:3] * dot(t_h[...], t_w[...]) - c_mod[s[2], 2:3] * dot(
                c_h[...], c_w[...]
            )
            keep_ref[...] = values[: image // 2]
            send_ref[...] = values[image // 2 :].astype(bf16)

        whole = pl.BlockSpec((image, score_units), lambda j: (0, 0))
        keep, send = pl.pallas_call(
            gap_body,
            grid=(width // tile,),
            in_specs=[pl.BlockSpec(memory_space=pltpu.SMEM), whole, whole]
            + [pl.BlockSpec((score_units, tile), lambda j: (0, j))] * 2
            + [pl.BlockSpec((*teacher_mod.shape[:2], tile), lambda j: (0, 0, j))] * 2,
            out_specs=[pl.BlockSpec((image // 2, tile), lambda j: (0, j))] * 2,
            out_shape=[shape(image // 2, width, dtype=f32), shape(image // 2, width)],
            compiler_params=pltpu.CompilerParams(vmem_limit_bytes=8 * 1024 * 1024),
            cost_estimate=pl.CostEstimate(
                flops=4 * image * width * score_units,
                bytes_accessed=4 * width * score_units,
                transcendentals=0,
            ),
            name="score_gap",
        )(scalars, teacher_hidden, critic_hidden, teacher_down, critic_down, teacher_mod, critic_mod)

        send, *input_tokens = settle(send, *input_tokens)
        input_tokens += [hop(values, "tp", core) for values in input_tokens]

        def gap_core_body(keep_ref, got_ref, send_ref, rest_ref):
            send_ref[...] = (keep_ref[rows:, :] + got_ref[rows:, :].astype(f32)).astype(bf16)
            rest_ref[...] = keep_ref[:rows, :] + got_ref[:rows, :].astype(f32)

        send, rest = kernel_call(
            gap_core_body,
            [shape(rows, width), shape(rows, width, dtype=f32)],
            keep,
            hop(send, "tp", core),
            name="gap_core",
        )

        def grad_body(s, rest_ref, got_ref, mod_ref, rows_ref, blocks_ref):
            level = (s[2].astype(f32) + 1.0) / level_count
            for m in masks:
                spot = block(s[0], m)
                gap = level * (rest_ref[:, spot] + got_ref[:, spot].astype(f32))
                values = (mod_ref[2:3, spot] * gap).astype(bf16)
                rows_ref[:, fixed(m)] = values
                blocks_ref[m] = values

        branch_grad, grad_blocks = kernel_call(
            grad_body,
            [shape(rows, width), shape(groups, rows, depth)],
            rest,
            hop(send, "tp", side),
            gen_mod,
            scalars=scalars,
            name="branch_grad",
        )

        branch_grad, grad_blocks, hidden_near[3], hidden_across[2] = settle(
            branch_grad, grad_blocks[None], hidden_near[3], hidden_across[2]
        )
        hidden_across.append(hop(hidden_near[3], "grp", swap))
        pair_grad = hop(branch_grad, "grp", pair)
        crossed = hop(branch_grad, "tp", side)
        arrived = send_blocks(grad_blocks, far)
        pair_grad, crossed, arrived = settle(pair_grad, crossed, arrived)
        pair_crossed = hop(pair_grad, "tp", side)
        own_tokens = [branch_grad, crossed]
        own_tokens += [hop(values, "tp", core) for values in own_tokens]
        grad_blocks = with_arrived(grad_blocks, arrived)
        arrived = send_blocks(grad_blocks, pair)
        pair_core = hop(pair_grad, "tp", core)
        pair_crossed, arrived, hidden_across[3] = settle(
            pair_crossed, arrived, hidden_across[3]
        )
        pair_tokens = [pair_grad, pair_crossed, pair_core, hop(pair_crossed, "tp", core)]

        def rows_grad_body(*refs):
            tokens, pieces = refs[:8], refs[8 : 8 + groups]
            pre_ref, out_ref, total = refs[8 + groups :]
            for m in masks:
                left = jnp.concatenate(
                    [t[:, fixed(m)] for t in tokens[:4]]
                    + [t[:, fixed(m ^ pair)] for t in tokens[4:]],
                    0,
                )
                term = dot(left, pieces[m][...], ((1,), (1,)))
                if m == 0:
                    total[...] = term
                else:
                    total[...] += term
            out_ref[...] = (total[...] * gate_slope(pre_ref[...])).astype(bf16)

        operands = (*own_tokens, *pair_tokens, *[down[m] for m in masks], gen_pre)
        rows_grad = pl.pallas_call(
            rows_grad_body,
            out_shape=shape(2 * image, units),
            in_specs=[pl.BlockSpec(memory_space=pltpu.VMEM) for _ in operands],
            out_specs=pl.BlockSpec(memory_space=pltpu.VMEM),
            scratch_shapes=[pltpu.VMEM((2 * image, units), f32)],
            compiler_params=pltpu.CompilerParams(vmem_limit_bytes=8 * 1024 * 1024),
            cost_estimate=pl.CostEstimate(
                flops=4 * image * width * units, bytes_accessed=10**7, transcendentals=0
            ),
            name="rows_grad",
        )(*operands)

        rows_grad, arrived = settle(rows_grad, arrived)
        near, across = [rows_grad, ring(rows_grad)], [hop(rows_grad, "grp", swap)]
        grad_blocks = with_arrived(grad_blocks, arrived)
        arrived = send_blocks(grad_blocks, swap)
        near[1], across[0], arrived = settle(near[1], across[0], arrived)
        near.append(ring(near[1]))
        across.append(hop(near[1], "grp", swap))
        grad_tokens = gather_tokens(with_arrived(grad_blocks, arrived)[:, 0])
        near[2], across[1], *grad_tokens = settle(near[2], across[1], *grad_tokens)
        near.append(ring(near[2]))
        across.append(hop(near[2], "grp", swap))
        input_columns = own_columns(input_tokens, scalars, (pair, far, swap))
        grad_columns = own_columns(grad_tokens, scalars, (far, pair, swap))

        def columns_at(table, k, other):
            origin = lax.rem(own + groups - 2 * k, groups) ^ other
            return lax.dynamic_index_in_dim(table, origin, 0, keepdims=False)

        def in_order(table, near, across, last=()):
            for k, piece in enumerate(near):
                yield k % 2, columns_at(table, k, 0), piece
            for k, piece in enumerate(across):
                yield k % 2, columns_at(table, k, swap), piece
            for at, piece in enumerate(last):
                columns = columns_at(table, groups // 2 - 1, swap)
                yield 1, columns[at * image : (at + 1) * image], piece

        def over_tokens(left, right):
            return dot(left, right, ((0,), (0,)))

        def join_halves(mine, other, axis):
            return jnp.where(
                half == 0,
                jnp.concatenate([mine, other], axis),
                jnp.concatenate([other, mine], axis),
            )

        down_sums = [0.0, 0.0]
        for which, columns, piece in in_order(
            grad_columns, hidden_near, hidden_across
        ):
            down_sums[which] += over_tokens(piece, columns)
        near[-1], across[-1], *down_sums = settle(near[-1], across[-1], *down_sums)
        last = [hop(near[-1][:image], "grp", swap), ring(across[-1][image:])]
        up_sums = [0.0, 0.0]
        for which, columns, piece in in_order(input_columns, near, across, last):
            up_sums[which] += over_tokens(columns, piece)
        return generated, join_halves(*up_sums, 1), join_halves(*down_sums, 0)

    return per_device


def make_per_device(groups, parts):
    def per_device(*args):
        depth, units = args[6].shape
        fits = depth % 128 == 0 and units % 512 == 0 and args[1].shape[1] % 16 == 0
        if groups == 8 and parts == 4 and fits:
            return make_paired(groups, parts)(*args)
        return make_ring(groups, parts)(*args)

    return per_device


def solution(mesh):
    in_specs = (
        P("grp", None, None),
        P("grp", "tp", None),
        P("grp"),
        P(),
        P(),
        P(),
        P("grp", "tp"),
        P("tp", "grp"),
        P(None, "tp"),
        P("tp", None),
        P(None, "tp"),
        P("tp", None),
    )
    out_specs = (P("grp", "tp", None), P("grp", "tp"), P("tp", "grp"))
    return jax.shard_map(
        make_per_device(mesh.shape["grp"], mesh.shape["tp"]),
        mesh=mesh,
        in_specs=in_specs,
        out_specs=out_specs,
        check_vma=False,
    )
```

```python
import jax
import jax.numpy as jnp
from jax import lax
from jax.experimental import pallas as pl
from jax.experimental.pallas import tpu as pltpu
from jax.sharding import PartitionSpec as P

epsilon = 1e-06
root_two_pi = 0.7978845608028654
cubic = 0.044715
f32 = jnp.float32
bf16 = jnp.bfloat16


def normalize(values):
    center = values - jnp.mean(values, axis=-1, keepdims=True)
    spread = jnp.mean(center * center, axis=-1, keepdims=True)
    return center * lax.rsqrt(spread + epsilon)


def smooth_gate(values):
    inner = root_two_pi * (values + cubic * values * values * values)
    return 0.5 * values * (1.0 + jnp.tanh(inner))


def gate_slope(values):
    inner = root_two_pi * (values + cubic * values * values * values)
    tangent = jnp.tanh(inner)
    return 0.5 * (1.0 + tangent) + 0.5 * values * (1.0 - tangent * tangent) * root_two_pi * (
        1.0 + 3.0 * cubic * values * values
    )


def pick_level(table, step_index):
    levels = lax.broadcasted_iota(jnp.int32, (table.shape[0], 1, 1), 0)
    return jnp.sum(jnp.where(levels == step_index, table, 0.0), axis=0)


def modulate(normed, picked):
    return (normed * (1.0 + picked[1]) + picked[0]).astype(bf16)


def dot(left, right, contract=((1,), (0,))):
    return lax.dot_general(left, right, (contract, ((), ())), preferred_element_type=f32)


def make_ring(groups, parts):
    places = groups // 2
    ring_pairs = [(2 * p + s, 2 * ((p + 1) % places) + s) for p in range(places) for s in range(2)]
    swap_pairs = [(g, g ^ 1) for g in range(groups)]

    def ring(piece):
        return lax.ppermute(piece, "grp", ring_pairs)

    def swap(piece):
        return lax.ppermute(piece, "grp", swap_pairs)

    def gather_groups(own):
        near, far = [own], []
        for _ in range(places - 1):
            far.append(swap(near[-1]))
            near.append(ring(near[-1]))
        half = own.shape[0] // 2
        first = swap(near[-1][:half])
        second = ring(far[-1][half:]) if far else swap(near[-1][half:])
        far.append(jnp.concatenate([first, second], axis=0))
        return near, far

    def bit_pairs(bit):
        return [(t, t ^ (1 << bit)) for t in range(parts)]

    bits = parts.bit_length() - 1

    def sum_parts(values):
        place = lax.axis_index("tp")
        blocks = values.reshape(parts, values.shape[0] // parts, values.shape[1])
        for bit in range(bits):
            mine = (place >> bit) & 1
            split = blocks.reshape(blocks.shape[0] // 2, 2, *blocks.shape[1:])
            keep = lax.dynamic_index_in_dim(split, mine, 1, keepdims=False)
            send = lax.dynamic_index_in_dim(split, 1 - mine, 1, keepdims=False)
            if bit > 0:
                send = send.astype(bf16)
            blocks = keep + lax.ppermute(send, "tp", bit_pairs(bit)).astype(f32)
        return blocks[0]

    def gather_parts(values):
        place = lax.axis_index("tp")
        blocks = values[None]
        for bit in reversed(range(bits)):
            mine = (place >> bit) & 1
            other = lax.ppermute(blocks, "tp", bit_pairs(bit))
            pair = jnp.where(
                mine == 0, jnp.stack([blocks, other], 1), jnp.stack([other, blocks], 1)
            )
            blocks = pair.reshape(-1, *values.shape)
        return blocks

    def per_device(
        gen_noise,
        diff_noise,
        timesteps,
        gen_mod,
        teacher_mod,
        critic_mod,
        gen_up,
        gen_down,
        teacher_up,
        teacher_down,
        critic_up,
        critic_down,
    ):
        local_rows = diff_noise.shape[1]
        depth = gen_up.shape[0]
        step_index = timesteps[0]
        own = lax.axis_index("grp")
        place, side = own // 2, own % 2
        own_start = lax.axis_index("tp") * local_rows

        def origins():
            for k in range(places):
                yield lax.rem(place - k + places, places) * 2 + side
            for k in range(places):
                yield lax.rem(place - k + places, places) * 2 + 1 - side

        def to_absolute(near, far):
            order = [(-r) % places for r in range(places)]
            pairs = [
                jnp.where(
                    side == 0,
                    jnp.concatenate([near[k], far[k]], 1),
                    jnp.concatenate([far[k], near[k]], 1),
                )
                for k in order
            ]
            both = jnp.concatenate(pairs + pairs[:-1], 1)
            width = pairs[0].shape[1]
            start = lax.rem(places - place, places) * width
            return lax.dynamic_slice_in_dim(both, start, width * places, 1)

        noise_all = gen_noise[0].astype(f32)
        gen_rows = modulate(normalize(noise_all), gen_mod)
        noise = lax.dynamic_slice_in_dim(noise_all, own_start, local_rows, 0)

        up_near, up_far = gather_groups(gen_up)
        down_near, down_far = gather_groups(gen_down)

        gen_pre = None
        for piece, origin in zip(up_near + up_far, origins()):
            term = dot(lax.dynamic_slice_in_dim(gen_rows, origin * depth, depth, 1), piece)
            gen_pre = term if gen_pre is None else gen_pre + term
        gen_hidden = smooth_gate(gen_pre).astype(bf16)

        branch_near = [dot(gen_hidden, piece) for piece in down_near]
        branch_far = [dot(gen_hidden, piece) for piece in down_far]
        partial = to_absolute(branch_near, branch_far)
        gen_branch = sum_parts(partial)

        generated = (noise + gen_mod[2] * gen_branch).astype(bf16)
        level = (step_index.astype(f32) + 1.0) / (teacher_mod.shape[0] + 1)
        noised = (
            (1.0 - level) * generated.astype(f32) + level * diff_noise[0].astype(f32)
        ).astype(bf16)
        teacher_row = pick_level(teacher_mod, step_index)
        critic_row = pick_level(critic_mod, step_index)
        noised_all = gather_parts(lax.optimization_barrier(noised)).reshape(
            noise_all.shape
        )
        normed = normalize(noised_all.astype(f32))

        def score(row, weight_up, weight_down):
            hidden = smooth_gate(dot(modulate(normed, row), weight_up)).astype(bf16)
            return row[2] * dot(hidden, weight_down)

        gap_part = score(teacher_row, teacher_up, teacher_down) - score(
            critic_row, critic_up, critic_down
        )
        gap = level * sum_parts(gap_part)
        branch_grad = (gen_mod[2] * gap).astype(bf16)

        def own_columns(rows):
            count = rows.shape[0]
            blocks = rows.reshape(count, groups, depth).transpose(1, 0, 2)
            blocks = lax.all_to_all(blocks, "grp", 0, 0, tiled=True)
            return gather_parts(blocks).transpose(1, 0, 2, 3).reshape(groups, -1, depth)

        input_columns = own_columns(
            lax.dynamic_slice_in_dim(gen_rows, own_start, local_rows, 0)
        )
        grad_columns = own_columns(branch_grad)

        hidden_near, hidden_far = gather_groups(gen_hidden)
        down_grad = None
        for piece, origin in zip(hidden_near + hidden_far, origins()):
            columns = lax.dynamic_index_in_dim(grad_columns, origin, 0, keepdims=False)
            term = dot(piece, columns, ((0,), (0,)))
            down_grad = term if down_grad is None else down_grad + term

        piece_grad = gather_parts(branch_grad).reshape(noise_all.shape)
        hidden_grad = None
        for piece, origin in zip(down_near + down_far, origins()):
            columns = lax.dynamic_slice_in_dim(piece_grad, origin * depth, depth, 1)
            term = dot(columns, piece, ((1,), (1,)))
            hidden_grad = term if hidden_grad is None else hidden_grad + term
        rows_grad = (hidden_grad * gate_slope(gen_pre)).astype(bf16)

        grad_near, grad_far = gather_groups(rows_grad)
        up_grad = None
        for piece, origin in zip(grad_near + grad_far, origins()):
            columns = lax.dynamic_index_in_dim(input_columns, origin, 0, keepdims=False)
            term = dot(columns, piece, ((0,), (0,)))
            up_grad = term if up_grad is None else up_grad + term
        return (generated[None], up_grad, down_grad)

    return per_device


def kernel_call(body, out_shapes, *operands, scalars=None, name, flops=0, moved=None):
    specs = [pl.BlockSpec(memory_space=pltpu.VMEM) for _ in operands]
    if scalars is not None:
        operands = (scalars, *operands)
        specs = [pl.BlockSpec(memory_space=pltpu.SMEM), *specs]
    total = sum(o.size * o.dtype.itemsize for o in operands)
    total += sum(o.size * jnp.dtype(o.dtype).itemsize for o in out_shapes)
    return pl.pallas_call(
        body,
        out_shape=tuple(out_shapes),
        in_specs=specs,
        out_specs=tuple(pl.BlockSpec(memory_space=pltpu.VMEM) for _ in out_shapes),
        compiler_params=pltpu.CompilerParams(vmem_limit_bytes=8 * 1024 * 1024),
        cost_estimate=pl.CostEstimate(flops=flops, bytes_accessed=total, transcendentals=0),
        name=name,
    )(*operands)


def settle(*arrays):
    def body(*refs):
        pass

    return pl.pallas_call(
        body,
        out_shape=tuple(jax.ShapeDtypeStruct(a.shape, a.dtype) for a in arrays),
        in_specs=[pl.BlockSpec(memory_space=pl.ANY) for _ in arrays],
        out_specs=tuple(pl.BlockSpec(memory_space=pl.ANY) for _ in arrays),
        input_output_aliases={i: i for i in range(len(arrays))},
        compiler_params=pltpu.CompilerParams(vmem_limit_bytes=256 * 1024),
        name="settle",
    )(*arrays)


def make_paired(groups, parts):
    pair, swap, far = 2, 1, 4
    core, side = 1, 2
    order = (0, side, core, core | side)
    masks = range(groups)

    def hop(values, axis, mask):
        size = groups if axis == "grp" else parts
        return lax.ppermute(values, axis, [(i, i ^ mask) for i in range(size)])

    def shape(*dims, dtype=bf16):
        return jax.ShapeDtypeStruct(dims, dtype)

    def gather_tokens(own):
        crossed = hop(own, "tp", side)
        return [own, crossed, hop(own, "tp", core), hop(crossed, "tp", core)]

    ring_pairs = [(g, (g + 2) % groups) for g in range(groups)]

    def ring(values):
        return lax.ppermute(values, "grp", ring_pairs)

    def send_blocks(blocks, mask):
        return hop(blocks[:, blocks.shape[1] // 2 :], "grp", mask)

    def with_arrived(blocks, arrived):
        return jnp.concatenate([blocks[:, : blocks.shape[1] // 2], arrived], 0)

    def own_columns(tokens, scalars, sent):
        _, rows, depth = tokens[0].shape

        def body(s, *refs):
            for g in masks:
                for at, image_index in enumerate((g, g ^ pair)):
                    m = s[0] ^ image_index
                    spot = sum(((m // bit) & 1) << place for place, bit in enumerate(sent))
                    for k, ref in enumerate(refs[:-1]):
                        start = (at * parts + k) * rows
                        refs[-1][g, start : start + rows, :] = ref[spot]

        (packed,) = kernel_call(
            body,
            [shape(groups, 2 * parts * rows, depth)],
            *tokens,
            scalars=scalars,
            name="pack",
        )
        return packed

    def per_device(
        gen_noise,
        diff_noise,
        timesteps,
        gen_mod,
        teacher_mod,
        critic_mod,
        gen_up,
        gen_down,
        teacher_up,
        teacher_down,
        critic_up,
        critic_down,
    ):
        rows = diff_noise.shape[1]
        image = gen_noise.shape[1]
        depth = gen_up.shape[0]
        width = gen_noise.shape[2]
        units = gen_up.shape[1] // 2
        middle = width // 2
        score_units = teacher_up.shape[1]
        level_count = teacher_mod.shape[0] + 1.0
        own = lax.axis_index("grp")
        part = lax.axis_index("tp")
        half = (own // pair) % 2
        scalars = jnp.stack([own, part, timesteps[0], half])

        def block(ref_own, m):
            return pl.ds(pl.multiple_of((ref_own ^ m) * depth, 128), depth)

        def fixed(m):
            return slice(m * depth, (m + 1) * depth)

        def halves(values, axis):
            return tuple(
                lax.dynamic_slice_in_dim(values, index * units, units, axis)
                for index in (half, 1 - half)
            )

        up, down = {}, {}
        up[0], up_send = halves(gen_up, 1)
        down[0], down_send = halves(gen_down, 0)

        def input_body(s, noise_ref, mod_ref, rows_ref, blocks_ref):
            for k, mask in enumerate(order):
                start = pl.multiple_of((s[1] ^ mask) * rows, 16)
                values = noise_ref[0, pl.ds(start, rows), :].astype(f32)
                values = normalize(values) * (1.0 + mod_ref[1:2]) + mod_ref[0:1]
                rows_ref[k * rows : (k + 1) * rows, :] = values.astype(bf16)
            for m in masks:
                place = (m & pair) * 2 + (m & far) // 2 + (m & swap)
                blocks_ref[place] = rows_ref[:rows, block(s[0], m)]

        up[pair] = hop(up_send, "grp", pair)
        up[far] = hop(up[0], "grp", far)
        up[swap] = hop(up[0], "grp", swap)
        gen_rows, input_blocks = kernel_call(
            input_body,
            [shape(image, width), shape(groups, rows, depth)],
            gen_noise,
            gen_mod,
            scalars=scalars,
            name="input",
        )
        (
            up[pair],
            up[far],
            up[swap],
            down_send,
            gen_rows,
            input_blocks,
        ) = settle(up[pair], up[far], up[swap], down_send, gen_rows, input_blocks)
        up[pair | far] = hop(up[pair], "grp", far)
        up[pair | swap] = hop(up[pair], "grp", swap)
        up[far | swap] = hop(up[far], "grp", swap)
        down[pair] = hop(down_send, "grp", pair)
        pair_rows = gather_tokens(hop(gen_rows[:rows], "grp", pair))
        (
            up[pair | far],
            up[pair | swap],
            up[far | swap],
            down[pair],
            down[0],
        ) = settle(up[pair | far], up[pair | swap], up[far | swap], down[pair], down[0])
        up[pair | far | swap] = hop(up[pair | far], "grp", swap)
        down[far] = hop(down[0], "grp", far)
        down[swap] = hop(down[0], "grp", swap)
        up[pair | far | swap], down[pair], down[far], down[swap], input_blocks = settle(
            up[pair | far | swap], down[pair], down[far], down[swap], input_blocks[None]
        )
        arrived = send_blocks(input_blocks, pair)
        down[pair | far] = hop(down[pair], "grp", far)
        down[pair | swap] = hop(down[pair], "grp", swap)
        down[far | swap] = hop(down[far], "grp", swap)

        def pre_body(s, rows_ref, p0, p1, p2, p3, *refs):
            pieces, (pre_ref, hidden_ref) = refs[:groups], refs[groups:]
            for m in masks:
                spot = block(s[0], m)
                left = jnp.concatenate(
                    [rows_ref[:, spot]] + [p[:, spot] for p in (p0, p1, p2, p3)], 0
                )
                term = dot(left, pieces[m][...])
                if m == 0:
                    pre_ref[...] = term
                else:
                    pre_ref[...] += term
            hidden_ref[...] = smooth_gate(pre_ref[...]).astype(bf16)

        gen_pre, gen_hidden = kernel_call(
            pre_body,
            [shape(2 * image, units, dtype=f32), shape(2 * image, units)],
            gen_rows,
            *pair_rows,
            *[up[m] for m in masks],
            scalars=scalars,
            name="pre",
            flops=4 * image * width * units,
        )

        def branch_body(hidden_ref, *refs):
            pieces, (keep_ref, send_ref) = refs[:-2], refs[-2:]
            for m, piece in enumerate(pieces):
                for image_at, spot in ((0, m), (1, m ^ pair)):
                    values = dot(
                        hidden_ref[image_at * image : (image_at + 1) * image, :], piece[...]
                    )
                    cut = slice(image_at * image // 2, (image_at + 1) * image // 2)
                    keep_ref[cut, fixed(spot)] = values[: image // 2]
                    send_ref[cut, fixed(spot)] = values[image // 2 :].astype(bf16)

        def core_body(keep_ref, got_ref, first_ref, second_ref, third_ref, rest_ref):
            def total(at):
                cut = slice(at * rows, (at + 1) * rows)
                return keep_ref[cut, :] + got_ref[cut, :].astype(f32)

            first_ref[...] = total(3).astype(bf16)
            second_ref[...] = total(1).astype(bf16)
            third_ref[...] = total(2)
            rest_ref[...] = total(0)

        def add_body(left_ref, right_ref, out_ref):
            out_ref[...] = (left_ref[...] + right_ref[...].astype(f32)).astype(bf16)

        def branch_core(which, hidden):
            count = groups // 2
            keep, send = kernel_call(
                branch_body,
                [shape(image, middle, dtype=f32), shape(image, middle)],
                hidden,
                *[down[m] for m in masks if m // count == which],
                name="branch",
                flops=2 * image * width * units,
            )
            return kernel_call(
                core_body,
                [shape(rows, middle)] * 2 + [shape(rows, middle, dtype=f32)] * 2,
                keep,
                hop(send, "tp", core),
                name="core_sum",
            )

        def branch_sum(first, second, third, rest):
            (third,) = kernel_call(
                add_body,
                [shape(rows, middle)],
                third,
                hop(first, "tp", side),
                name="side_sum",
            )
            return rest, hop(second, "tp", side), hop(third, "grp", pair)

        (
            down[pair | far],
            down[pair | swap],
            down[far | swap],
            gen_hidden,
            arrived,
        ) = settle(
            down[pair | far],
            down[pair | swap],
            down[far | swap],
            gen_hidden,
            arrived,
        )
        input_blocks = with_arrived(input_blocks, arrived)
        down[pair | far | swap] = hop(down[pair | far], "grp", swap)
        arrived = send_blocks(input_blocks, far)
        left_terms = branch_core(0, gen_hidden)
        down[pair | far | swap], gen_hidden, arrived, *left_terms = settle(
            down[pair | far | swap], gen_hidden, arrived, *left_terms
        )
        left_sum = branch_sum(*left_terms)
        hidden_near = [gen_hidden, ring(gen_hidden)]
        hidden_across = [hop(gen_hidden, "grp", swap)]
        right_sum = branch_sum(*branch_core(1, gen_hidden))

        def latent_body(s, noise_ref, diff_ref, mod_ref, *refs):
            sums, (generated_ref, noised_ref) = refs[:6], refs[6:]
            level = (s[2].astype(f32) + 1.0) / level_count
            start = pl.multiple_of(s[1] * rows, 16)
            for m in masks:
                which, at = divmod(m, groups // 2)
                a, b, c = sums[3 * which : 3 * which + 3]
                branch = (
                    a[:, fixed(at)] + b[:, fixed(at)].astype(f32) + c[:, fixed(at)].astype(f32)
                )
                spot = block(s[0], m)
                noise = noise_ref[0, pl.ds(start, rows), spot].astype(f32)
                made = (noise + mod_ref[2:3, spot] * branch).astype(bf16)
                generated_ref[0, :, spot] = made
                noised_ref[:, spot] = (
                    (1.0 - level) * made.astype(f32) + level * diff_ref[0, :, spot].astype(f32)
                ).astype(bf16)

        generated, noised = kernel_call(
            latent_body,
            [shape(1, rows, width), shape(rows, width)],
            gen_noise,
            diff_noise,
            gen_mod,
            *left_sum,
            *right_sum,
            scalars=scalars,
            name="latent",
        )

        noised, hidden_near[1], hidden_across[0], arrived = settle(
            noised, hidden_near[1], hidden_across[0], arrived
        )
        hidden_near.append(ring(hidden_near[1]))
        hidden_across.append(hop(hidden_near[1], "grp", swap))
        input_blocks = with_arrived(input_blocks, arrived)
        arrived = send_blocks(input_blocks, swap)

        def score_input_body(s, n0, n1, n2, n3, teacher_ref, critic_ref, t_ref, c_ref):
            for k, part_ref in enumerate((n0, n1, n2, n3)):
                normed = normalize(part_ref[...].astype(f32))
                cut = slice(k * rows, (k + 1) * rows)
                for table, out in ((teacher_ref, t_ref), (critic_ref, c_ref)):
                    row = table[s[2]]
                    out[cut, :] = (normed * (1.0 + row[1:2]) + row[0:1]).astype(bf16)

        teacher_in, critic_in = kernel_call(
            score_input_body,
            [shape(image, width)] * 2,
            *gather_tokens(noised),
            teacher_mod,
            critic_mod,
            scalars=scalars,
            name="score_input",
        )


        tile = 256

        def hidden_body(t_in, c_in, t_w, c_w, t_out, c_out):
            t_out[...] = smooth_gate(dot(t_in[...], t_w[...])).astype(bf16)
            c_out[...] = smooth_gate(dot(c_in[...], c_w[...])).astype(bf16)

        whole = pl.BlockSpec((image, width), lambda j: (0, 0))
        teacher_hidden, critic_hidden = pl.pallas_call(
            hidden_body,
            grid=(score_units // tile,),
            in_specs=[whole, whole] + [pl.BlockSpec((width, tile), lambda j: (0, j))] * 2,
            out_specs=[pl.BlockSpec((image, tile), lambda j: (0, j))] * 2,
            out_shape=[shape(image, score_units)] * 2,
            compiler_params=pltpu.CompilerParams(vmem_limit_bytes=8 * 1024 * 1024),
            cost_estimate=pl.CostEstimate(
                flops=4 * image * width * score_units,
                bytes_accessed=4 * width * score_units,
                transcendentals=0,
            ),
            name="score_hidden",
        )(teacher_in, critic_in, teacher_up, critic_up)

        teacher_hidden, hidden_near[2], hidden_across[1], arrived = settle(
            teacher_hidden, hidden_near[2], hidden_across[1], arrived
        )
        hidden_near.append(ring(hidden_near[2]))
        hidden_across.append(hop(hidden_near[2], "grp", swap))
        input_tokens = [with_arrived(input_blocks, arrived)[:, 0]]
        input_tokens.append(hop(input_tokens[0], "tp", side))

        def gap_body(s, t_h, c_h, t_w, c_w, t_mod, c_mod, keep_ref, send_ref):
            values = t_mod[s[2], 2:3] * dot(t_h[...], t_w[...]) - c_mod[s[2], 2:3] * dot(
                c_h[...], c_w[...]
            )
            keep_ref[...] = values[: image // 2]
            send_ref[...] = values[image // 2 :].astype(bf16)

        whole = pl.BlockSpec((image, score_units), lambda j: (0, 0))
        keep, send = pl.pallas_call(
            gap_body,
            grid=(width // tile,),
            in_specs=[pl.BlockSpec(memory_space=pltpu.SMEM), whole, whole]
            + [pl.BlockSpec((score_units, tile), lambda j: (0, j))] * 2
            + [pl.BlockSpec((*teacher_mod.shape[:2], tile), lambda j: (0, 0, j))] * 2,
            out_specs=[pl.BlockSpec((image // 2, tile), lambda j: (0, j))] * 2,
            out_shape=[shape(image // 2, width, dtype=f32), shape(image // 2, width)],
            compiler_params=pltpu.CompilerParams(vmem_limit_bytes=8 * 1024 * 1024),
            cost_estimate=pl.CostEstimate(
                flops=4 * image * width * score_units,
                bytes_accessed=4 * width * score_units,
                transcendentals=0,
            ),
            name="score_gap",
        )(scalars, teacher_hidden, critic_hidden, teacher_down, critic_down, teacher_mod, critic_mod)

        send, *input_tokens = settle(send, *input_tokens)
        input_tokens += [hop(values, "tp", core) for values in input_tokens]

        def gap_core_body(keep_ref, got_ref, send_ref, rest_ref):
            send_ref[...] = (keep_ref[rows:, :] + got_ref[rows:, :].astype(f32)).astype(bf16)
            rest_ref[...] = keep_ref[:rows, :] + got_ref[:rows, :].astype(f32)

        send, rest = kernel_call(
            gap_core_body,
            [shape(rows, width), shape(rows, width, dtype=f32)],
            keep,
            hop(send, "tp", core),
            name="gap_core",
        )

        def grad_body(s, rest_ref, got_ref, mod_ref, rows_ref, blocks_ref):
            level = (s[2].astype(f32) + 1.0) / level_count
            for m in masks:
                spot = block(s[0], m)
                gap = level * (rest_ref[:, spot] + got_ref[:, spot].astype(f32))
                values = (mod_ref[2:3, spot] * gap).astype(bf16)
                rows_ref[:, fixed(m)] = values
                blocks_ref[m] = values

        branch_grad, grad_blocks = kernel_call(
            grad_body,
            [shape(rows, width), shape(groups, rows, depth)],
            rest,
            hop(send, "tp", side),
            gen_mod,
            scalars=scalars,
            name="branch_grad",
        )

        branch_grad, grad_blocks, hidden_near[3], hidden_across[2] = settle(
            branch_grad, grad_blocks[None], hidden_near[3], hidden_across[2]
        )
        hidden_across.append(hop(hidden_near[3], "grp", swap))
        pair_grad = hop(branch_grad, "grp", pair)
        crossed = hop(branch_grad, "tp", side)
        arrived = send_blocks(grad_blocks, far)
        pair_grad, crossed, arrived = settle(pair_grad, crossed, arrived)
        pair_crossed = hop(pair_grad, "tp", side)
        own_tokens = [branch_grad, crossed]
        own_tokens += [hop(values, "tp", core) for values in own_tokens]
        grad_blocks = with_arrived(grad_blocks, arrived)
        arrived = send_blocks(grad_blocks, pair)
        pair_core = hop(pair_grad, "tp", core)
        pair_crossed, arrived, hidden_across[3] = settle(
            pair_crossed, arrived, hidden_across[3]
        )
        pair_tokens = [pair_grad, pair_crossed, pair_core, hop(pair_crossed, "tp", core)]
        grad_blocks = with_arrived(grad_blocks, arrived)
        arrived = send_blocks(grad_blocks, swap)

        def rows_grad_body(*refs):
            tokens, pieces = refs[:8], refs[8 : 8 + groups]
            pre_ref, out_ref, total = refs[8 + groups :]
            for m in masks:
                left = jnp.concatenate(
                    [t[:, fixed(m)] for t in tokens[:4]]
                    + [t[:, fixed(m ^ pair)] for t in tokens[4:]],
                    0,
                )
                term = dot(left, pieces[m][...], ((1,), (1,)))
                if m == 0:
                    total[...] = term
                else:
                    total[...] += term
            out_ref[...] = (total[...] * gate_slope(pre_ref[...])).astype(bf16)

        operands = (*own_tokens, *pair_tokens, *[down[m] for m in masks], gen_pre)
        rows_grad = pl.pallas_call(
            rows_grad_body,
            out_shape=shape(2 * image, units),
            in_specs=[pl.BlockSpec(memory_space=pltpu.VMEM) for _ in operands],
            out_specs=pl.BlockSpec(memory_space=pltpu.VMEM),
            scratch_shapes=[pltpu.VMEM((2 * image, units), f32)],
            compiler_params=pltpu.CompilerParams(vmem_limit_bytes=8 * 1024 * 1024),
            cost_estimate=pl.CostEstimate(
                flops=4 * image * width * units, bytes_accessed=10**7, transcendentals=0
            ),
            name="rows_grad",
        )(*operands)

        rows_grad, arrived = settle(rows_grad, arrived)
        near, across = [rows_grad, ring(rows_grad)], [hop(rows_grad, "grp", swap)]
        near[1], across[0], arrived = settle(near[1], across[0], arrived)
        near.append(ring(near[1]))
        across.append(hop(near[1], "grp", swap))
        grad_tokens = gather_tokens(with_arrived(grad_blocks, arrived)[:, 0])
        near[2], across[1], *grad_tokens = settle(near[2], across[1], *grad_tokens)
        near.append(ring(near[2]))
        across.append(hop(near[2], "grp", swap))
        input_columns = own_columns(input_tokens, scalars, (pair, far, swap))
        grad_columns = own_columns(grad_tokens, scalars, (far, pair, swap))

        def columns_at(table, k, other):
            origin = lax.rem(own + groups - 2 * k, groups) ^ other
            return lax.dynamic_index_in_dim(table, origin, 0, keepdims=False)

        def in_order(table, near, across, last=()):
            for k, piece in enumerate(near):
                yield k % 2, columns_at(table, k, 0), piece
            for k, piece in enumerate(across):
                yield k % 2, columns_at(table, k, swap), piece
            for at, piece in enumerate(last):
                columns = columns_at(table, groups // 2 - 1, swap)
                yield 1, columns[at * image : (at + 1) * image], piece

        def over_tokens(left, right):
            return dot(left, right, ((0,), (0,)))

        def join_halves(mine, other, axis):
            return jnp.where(
                half == 0,
                jnp.concatenate([mine, other], axis),
                jnp.concatenate([other, mine], axis),
            )

        down_sums = [0.0, 0.0]
        for which, columns, piece in in_order(
            grad_columns, hidden_near, hidden_across
        ):
            down_sums[which] += over_tokens(piece, columns)
        near[-1], across[-1], *down_sums = settle(near[-1], across[-1], *down_sums)
        last = [hop(near[-1][:image], "grp", swap), ring(across[-1][image:])]
        up_sums = [0.0, 0.0]
        for which, columns, piece in in_order(input_columns, near, across, last):
            up_sums[which] += over_tokens(columns, piece)
        return generated, join_halves(*up_sums, 1), join_halves(*down_sums, 0)

    return per_device


def make_per_device(groups, parts):
    def per_device(*args):
        depth, units = args[6].shape
        fits = depth % 128 == 0 and units % 512 == 0 and args[1].shape[1] % 16 == 0
        if groups == 8 and parts == 4 and fits:
            return make_paired(groups, parts)(*args)
        return make_ring(groups, parts)(*args)

    return per_device


def solution(mesh):
    in_specs = (
        P("grp", None, None),
        P("grp", "tp", None),
        P("grp"),
        P(),
        P(),
        P(),
        P("grp", "tp"),
        P("tp", "grp"),
        P(None, "tp"),
        P("tp", None),
        P(None, "tp"),
        P("tp", None),
    )
    out_specs = (P("grp", "tp", None), P("grp", "tp"), P("tp", "grp"))
    return jax.shard_map(
        make_per_device(mesh.shape["grp"], mesh.shape["tp"]),
        mesh=mesh,
        in_specs=in_specs,
        out_specs=out_specs,
        check_vma=False,
    )
```
